512 devices in a mesh: stream: 64 (over y, z), span: 8 (over x, core).
Axes of the slice: x: 4, y: 8, z: 8, core: 2. Of those that a mesh axis runs over, the one named last changes fastest.
Arguments:
- solution: float32 [80, 4, 128, 8, 128], P(None, None, 'stream', 'span'), may hold values from -6 to 6
- forcing: float32 [80, 4, 128, 8, 128], P(None, None, 'stream', 'span'), may hold values from -6 to 6
- pseudo_shift: float32 [128, 8, 128], P('stream', 'span'), may hold values from 0.02 to 0.2
- stream_faces: float32 [128, 8, 128], P('stream', 'span'), may hold values from 5 to 50
- span_faces: float32 [128, 8, 128], P('stream', 'span'), may hold values from 0.05 to 0.5
- normal_faces: float32 [128, 8, 128], P('stream', 'span'), may hold values from 0.05 to 0.5
- coupling_span: float32 [80, 80], replicated, may hold values from -0.625 to 0.625
- coupling_normal: float32 [80, 80], replicated, may hold values from -0.625 to 0.625
- reflectors: float32 [8, 80], replicated, may hold values from -6 to 6
- eigenvalues: float32 [80], replicated, may hold values from -1 to 1
- line_start: int32 [8, 128], P('span'), may hold values from 0 to 112, as said below
- line_length: int32 [8, 128], P('span'), may hold values from 16 to 128
- line_order: int32 [8, 128], P('span'), may hold values from 0 to 127, each once within a row
Outputs:
- relaxed: float32 [80, 4, 128, 8, 128], P(None, None, 'stream', 'span')
- line_states: float32 [80, 4, 1024, 128], P(None, None, ('span', 'stream'))
The draws below stay inside these ranges and needn't reach their ends.
Inputs may be any that keep to these rules, and one draw needn't show every extreme that they name: Each line ends inside the grid: line_start + line_length <= 128. `line_order`: each row lists every line of its spanwise tile once; slot j belongs to the stream device j // 2.
All inputs are finite; a program needn't handle non-finite values.
Results may differ from the reference program's by a relative error of at most 0.0003.
Values sent between devices are 32-bit elements; how exact they have to be, the bound alone decides.
A program may use at most 128 MiB of HBM per device.

```python
import math
import jax
import jax.numpy as jnp
from jax import lax

V = 80
R = 4
REFLECT = 8
CZ = 1
NN = 128
NS = 128
NZ = 8
LT = 128
N_SPAN = 8


def rim_tables(key):
    base = jax.random.fold_in(key, 11)
    line_total = NZ * NN
    length_key, start_key, pick_key, other_key = jax.random.split(base, 4)
    lengths = jax.random.randint(length_key, (line_total,), NS // 8, NS + 1)
    longest = jax.random.randint(pick_key, (), 0, line_total)
    shortest = (longest + 1 + jax.random.randint(other_key, (), 0, line_total - 1)) % line_total
    lengths = lengths.at[longest].set(NS).at[shortest].set(NS // 8)
    spare_room = NS - lengths + 1
    starts = jax.random.randint(start_key, (line_total,), 0, 1 << 20) % spare_room
    starts = starts.at[longest].set(0).at[shortest].set(NS - NS // 8)
    return (starts.reshape(NZ, NN).astype(jnp.int32), lengths.reshape(NZ, NN).astype(jnp.int32))


def draw_line_start(key, part):
    return rim_tables(key)[0]


def draw_line_length(key, part):
    return rim_tables(key)[1]


def steps_of(key, extent, shards, low, largest):
    loudness = 1.0
    for position, shards_of in shards:
        draws = jax.random.uniform(jax.random.fold_in(jax.random.fold_in(key, 6), position), (shards_of,), jnp.float32, low / len(shards), largest / len(shards))
        loudness = loudness * jnp.repeat(jnp.exp(draws), extent[position] // shards_of).reshape((-1,) + (1,) * (len(extent) - 1 - position))
    return loudness


def centred(stream_key, extent, scale, most, shards=(), kind=jnp.bfloat16):
    loudness = steps_of(stream_key, extent, shards, -0.22, 0.18) if shards else 1.0
    values = jax.random.normal(stream_key, extent, jnp.float32) * scale * loudness
    return jnp.minimum(jnp.maximum(values, -most), most).astype(kind)


def setup_inputs(seed: int = 0) -> dict:
    arg_keys = jax.random.split(jax.random.key(seed), 14)
    solution = centred(arg_keys[0], (V, R, NS, NZ, NN), 1.0, 6.0, ((2, 64), (3, 8)), jnp.float32)
    forcing = centred(arg_keys[1], (V, R, NS, NZ, NN), 1.0, 6.0, ((2, 64), (3, 8)), jnp.float32)
    pseudo_shift = jnp.clip(jnp.exp(math.log(0.2) - 2.3025851 * jax.random.uniform(arg_keys[2], (NS, NZ, NN), jnp.float32) ** steps_of(arg_keys[2], (NS, NZ, NN), ((0, 64), (1, 8)), -0.2, 0.2)), 0.02, 0.2)
    stream_faces = jnp.clip(jnp.exp(math.log(50.0) - 2.3025851 * jax.random.uniform(arg_keys[3], (NS, NZ, NN), jnp.float32) ** steps_of(arg_keys[3], (NS, NZ, NN), ((0, 64), (1, 8)), -0.2, 0.2)), 5.0, 50.0)
    span_faces = jnp.clip(jnp.exp(math.log(0.5) - 2.3025851 * jax.random.uniform(arg_keys[4], (NS, NZ, NN), jnp.float32) ** steps_of(arg_keys[4], (NS, NZ, NN), ((0, 64), (1, 8)), -0.2, 0.2)), 0.05, 0.5)
    normal_faces = jnp.clip(jnp.exp(math.log(0.5) - 2.3025851 * jax.random.uniform(arg_keys[5], (NS, NZ, NN), jnp.float32) ** steps_of(arg_keys[5], (NS, NZ, NN), ((0, 64), (1, 8)), -0.2, 0.2)), 0.05, 0.5)
    coupling_span = centred(arg_keys[6], (V, V), V ** -0.5, 0.625, (), jnp.float32)
    coupling_normal = centred(arg_keys[7], (V, V), V ** -0.5, 0.625, (), jnp.float32)
    reflectors = centred(arg_keys[8], (REFLECT, V), 1.0, 6.0, (), jnp.float32)
    eigenvalues = jnp.clip(jax.random.uniform(arg_keys[9], (V,), jnp.float32, -1.0, 1.0), -1.0, 1.0)
    line_start = draw_line_start(jax.random.fold_in(arg_keys[13], 71), 0)
    line_length = draw_line_length(jax.random.fold_in(arg_keys[13], 71), 0)
    line_order = jax.vmap(lambda own: jax.random.permutation(own, LT))(jax.random.split(arg_keys[12], N_SPAN)).reshape((N_SPAN, LT)).astype(jnp.int32)
    return {"solution": solution, "forcing": forcing, "pseudo_shift": pseudo_shift, "stream_faces": stream_faces, "span_faces": span_faces, "normal_faces": normal_faces, "coupling_span": coupling_span, "coupling_normal": coupling_normal, "reflectors": reflectors, "eigenvalues": eigenvalues, "line_start": line_start, "line_length": line_length, "line_order": line_order}


def build_modes(reflectors, eigenvalues):
    eigen_basis = jnp.eye(eigenvalues.shape[0], dtype=eigenvalues.dtype)
    for number in range(reflectors.shape[0]):
        vector = reflectors[number]
        factor = 2.0 / (jnp.sum(vector * vector) + 1e-6)
        projected = jnp.dot(eigen_basis, vector, precision=lax.Precision.HIGHEST)
        eigen_basis = eigen_basis - factor * projected[:, None] * vector[None, :]
    coupling = jnp.dot(eigen_basis * eigenvalues[None, :], eigen_basis.T, precision=lax.Precision.HIGHEST)
    absolute = jnp.dot(eigen_basis * jnp.abs(eigenvalues)[None, :], eigen_basis.T, precision=lax.Precision.HIGHEST)
    return eigen_basis, coupling, absolute


def apply_block(matrix, field):
    return jnp.tensordot(matrix, field, axes=1, precision=lax.Precision.HIGHEST)


def previous(field, axis):
    widths = [(0, 0)] * field.ndim
    widths[axis] = (1, 0)
    return lax.slice_in_dim(jnp.pad(field, widths), 0, field.shape[axis], axis=axis)


def following(field, axis):
    widths = [(0, 0)] * field.ndim
    widths[axis] = (0, 1)
    return lax.slice_in_dim(jnp.pad(field, widths), 1, field.shape[axis] + 1, axis=axis)


def thomas(lower_band, main_band, upper_band, right_side):
    def forward(carry, items):
        prev_upper, prev_rhs = carry
        low_item, mid_item, up_item, rhs_item = items
        denominator = mid_item - low_item * prev_upper
        new_upper = up_item / denominator
        new_rhs = (rhs_item - low_item * prev_rhs) / denominator
        return (new_upper, new_rhs), (new_upper, new_rhs)

    start = (jnp.zeros_like(upper_band[0]), jnp.zeros_like(right_side[0]))
    unused, (uppers, rhss) = lax.scan(forward, start, (lower_band, main_band, upper_band, right_side))

    def backward(later, items):
        up_item, rhs_item = items
        value = rhs_item - up_item * later
        return value, value

    unused_last, solved = lax.scan(backward, jnp.zeros_like(right_side[0]), (uppers, rhss), reverse=True)
    return solved


def reference(solution, forcing, pseudo_shift, stream_faces, span_faces, normal_faces, coupling_span, coupling_normal, reflectors, eigenvalues, line_start, line_length, line_order):
    eigen_basis, coupling, absolute = build_modes(reflectors, eigenvalues)
    stream_pos = jnp.arange(NS, dtype=jnp.int32)[:, None, None]
    active = (stream_pos >= line_start[None]) & (stream_pos + 1 < line_start[None] + line_length[None])
    stream_face = jnp.where(active, stream_faces, 0.0)
    stream_left = previous(stream_face, 0)
    span_left = jnp.roll(span_faces, 1, axis=1)
    normal_pos = jnp.arange(NN, dtype=jnp.int32)
    normal_face = jnp.where(normal_pos < NN - 1, normal_faces, 0.0)
    normal_left = previous(normal_face, 2)
    diag_shift = pseudo_shift + span_left + span_faces + normal_left + normal_face
    offline = apply_block(coupling_span, span_left * jnp.roll(solution, 1, axis=3) + span_faces * jnp.roll(solution, -1, axis=3))
    offline = offline + apply_block(coupling_normal, normal_left * previous(solution, 4) + normal_face * following(solution, 4))
    line_part = apply_block(absolute, (stream_left + stream_face) * solution)
    line_part = line_part - apply_block(coupling, stream_left * previous(solution, 2) + stream_face * following(solution, 2))
    residual = forcing - diag_shift * solution - line_part + offline
    modal_rhs = apply_block(eigen_basis.T, residual)
    mode_rate = eigenvalues[:, None, None, None]
    lower_band = -mode_rate * stream_left[:, None, None]
    upper_band = -mode_rate * stream_face[:, None, None]
    main_band = diag_shift[:, None, None] + jnp.abs(mode_rate) * (stream_left + stream_face)[:, None, None]
    solved = thomas(lower_band, main_band, upper_band, jnp.moveaxis(modal_rhs, 2, 0))
    relaxed = solution + apply_block(eigen_basis, jnp.moveaxis(solved, 0, 2))
    line_total = CZ * NN
    slot_index = (jnp.arange(N_SPAN, dtype=jnp.int32)[:, None] * line_total + line_order).reshape(-1)
    flattened = relaxed.reshape(relaxed.shape[0], relaxed.shape[1], NS, NZ * NN)
    line_states = jnp.take(flattened, slot_index, axis=3).transpose(0, 1, 3, 2)
    return relaxed, line_states
```

```python
import functools

import jax
import jax.numpy as jnp
from jax import lax
from jax.experimental import pallas as pl
from jax.experimental.pallas import tpu as pltpu
from jax.sharding import PartitionSpec as P

F32 = jnp.float32
BF16 = jnp.bfloat16
MESH = pl.DeviceIdType.MESH
EPS = 1e-06


def iota(shape, dim):
    return lax.broadcasted_iota(jnp.int32, shape, dim)


def split(x):
    high = x.astype(BF16)
    return high, (x - high.astype(F32)).astype(BF16)


def split3(x):
    high = x.astype(BF16)
    rest = x - high.astype(F32)
    mid = rest.astype(BF16)
    return high, mid, (rest - mid.astype(F32)).astype(BF16)


def dot(a, b, ca=1, cb=0):
    return lax.dot_general(a, b, (((ca,), (cb,)), ((), ())), preferred_element_type=F32)


def dot3(a, b, ca=1, cb=0):
    ah, al = split(a)
    bh, bl = split(b)
    return dot(ah, bh, ca, cb) + (dot(al, bh, ca, cb) + dot(ah, bl, ca, cb))


def body(
    sol, frc, pse, stf, spf, nof, cs, cn, reflectors, lam, start, length, order,
    out_rel, out_ls,
    pse_ref, stf_ref, nof_ref, cs_ref, cn_ref, refl_ref, lam_ref, start_ref, length_ref, order_ref,
    u_buf, ul_buf, ur_buf, f_buf, spf_send, spl_recv, m2_send, m2l_recv, m2r_recv,
    e_send, e_recv, g_send, g_recv, y_send, y_recv,
    pad_buf, da_buf, db_buf, f0_buf, f1_buf, inv_buf, a_buf, b_buf, d_buf, rel_buf, ls_buf,
    loc_sem, out_sem, halo_send_sem, halo_recv_sem, tiny_send_sem, tiny_recv_sem,
    e_sems, gs_sem, gr_sem, ys_sem, yr_sem,
):
    me = lax.axis_index("stream")
    count = lax.axis_size("stream")
    sp = lax.axis_index("span")
    sp_count = lax.axis_size("span")
    sp_left = lax.rem(sp + sp_count - 1, sp_count)
    sp_right = lax.rem(sp + 1, sp_count)
    st_left = lax.rem(me + count - 1, count)
    st_right = lax.rem(me + 1, count)

    loads_u = [
        pltpu.make_async_copy(sol.at[:, rs // 2, rs % 2, 0, :], u_buf.at[rs], loc_sem.at[rs]) for rs in range(8)
    ]
    loads_f = [
        pltpu.make_async_copy(frc.at[:, rs // 2, rs % 2, 0, :], f_buf.at[rs], loc_sem.at[8 + rs]) for rs in range(8)
    ]
    first = ((order, order_ref), (spf.at[:, 0], spf_send), (reflectors, refl_ref), (lam, lam_ref))
    later = (
        (cs, cs_ref), (cn, cn_ref), (pse.at[:, 0], pse_ref), (stf.at[:, 0], stf_ref), (nof.at[:, 0], nof_ref),
        (start, start_ref), (length, length_ref),
    )
    loads_small = [
        pltpu.make_async_copy(src, dst, loc_sem.at[16 + i]) for i, (src, dst) in enumerate(first + later)
    ]
    for load in loads_small[:4]:
        load.start()
    for load in loads_u:
        load.start()
    for load in loads_small[4:]:
        load.start()
    for load in loads_f:
        load.start()
    g_recv[...] = jnp.zeros_like(g_recv)

    barrier = pltpu.get_barrier_semaphore()
    for side in (sp_left, sp_right):
        pl.semaphore_signal(barrier, inc=1, device_id={"span": side}, device_id_type=MESH)

    def greet(i, carry):
        pl.semaphore_signal(
            barrier, inc=1, device_id={"stream": lax.rem(me + i, count)}, device_id_type=MESH
        )
        return carry

    lax.fori_loop(1, count, greet, 0)

    for load in loads_small[:4]:
        load.wait()

    lane = iota((128, 128), 1)
    row = iota((128, 128), 0)
    perm_t = jnp.where(row == order_ref[...], 1.0, 0.0).astype(BF16)
    pair_line = row // 64
    pick = jnp.where(lane == 2 * (row - 64 * pair_line) + pair_line, 1.0, 0.0).astype(BF16)
    perm = dot(pick, perm_t, 1, 1).astype(BF16)

    for load in loads_u:
        load.wait()
    pl.semaphore_wait(barrier, count + 1)

    halos = []
    for c in range(2):
        for k, (side, buf) in enumerate(((sp_right, ul_buf), (sp_left, ur_buf))):
            halo = pltpu.make_async_remote_copy(
                u_buf.at[pl.ds(4 * c, 4)],
                buf.at[pl.ds(4 * c, 4)],
                halo_send_sem.at[2 * c + k],
                halo_recv_sem.at[2 * c + k],
                device_id={"span": side},
                device_id_type=MESH,
            )
            if c == 0 and k == 0:
                spf_halo = pltpu.make_async_remote_copy(
                    spf_send, spl_recv, tiny_send_sem.at[0], tiny_recv_sem.at[0],
                    device_id={"span": sp_right}, device_id_type=MESH,
                )
                spf_halo.start()
            halo.start()
            halos.append(halo)

    for load in loads_small[4:]:
        load.wait()

    pad_buf[...] = jnp.zeros_like(pad_buf)
    pad_buf[0:8, 0:80] = refl_ref[...]
    pad_buf[8:9, 0:80] = lam_ref[...]
    refl = pad_buf[0:8, :]
    lam_row = pad_buf[8:9, :]
    norms = jnp.sum(refl * refl, axis=1, keepdims=True)
    factors = 2.0 / (norms + EPS)
    scales = 2.0 * (EPS**0.5) / (norms + EPS)
    lane80 = iota((80, 128), 1)
    row8 = iota((8, 128), 0)
    basis = jnp.where(iota((80, 128), 0) == lane80, 1.0, 0.0)
    side_z = jnp.zeros((80, 128), F32)
    side_p = jnp.zeros((8, 128), F32)
    for k in range(8):
        w = refl[k : k + 1, :]
        factor = factors[k : k + 1, :]
        z = jnp.sum(basis * w, axis=1, keepdims=True)
        basis = basis - (factor * z) * w
        side_z = jnp.where(lane80 == 80 + k, z * scales[k : k + 1, :], side_z)
        side_p = side_p - (factor * jnp.sum(side_p * w, axis=1, keepdims=True)) * w
        side_p = jnp.where(row8 == k, w, side_p)
    side_p = side_p * scales
    basis_z = basis + side_z
    zt = jnp.transpose(jnp.concatenate([basis_z, jnp.zeros((48, 128), F32)], axis=0))[80:88, 0:80]
    m1 = dot3(side_p * jnp.abs(lam_row), basis, 1, 1)
    m2 = dot3(side_p * lam_row, basis, 1, 1)
    small = jnp.concatenate([m1, m2, zt], axis=0)
    state = jnp.concatenate([u_buf[rs] for rs in range(8)], axis=1)
    small_u = dot3(small, state)

    def part(base, r, s):
        rs = 2 * r + s
        return small_u[base : base + 8, rs * 128 : rs * 128 + 128]

    for s in range(2):
        for r in range(4):
            m2_send[s, 8 * r : 8 * r + 8, :] = part(8, r, s)
        m2_send[s, 32:40, :] = jnp.broadcast_to(stf_ref[s : s + 1, :], (8, 128))
    m2_halos = [
        pltpu.make_async_remote_copy(
            m2_send.at[1 - k], buf, tiny_send_sem.at[1 + k], tiny_recv_sem.at[1 + k],
            device_id={"stream": side}, device_id_type=MESH,
        )
        for k, (side, buf) in enumerate(((st_right, m2l_recv), (st_left, m2r_recv)))
    ]
    for halo in m2_halos:
        halo.start()

    line_start = start_ref[...]
    line_end = line_start + length_ref[...]

    def masked(faces, pos):
        return jnp.where((pos >= line_start) & (pos + 1 < line_end), faces, 0.0)

    face = [masked(stf_ref[s : s + 1, :], 2 * me + s) for s in range(2)]
    lane1 = iota((1, 128), 1)
    normal_face = [jnp.where(lane1 < 127, nof_ref[s : s + 1, :], 0.0) for s in range(2)]
    normal_left = [jnp.where(lane1 > 0, pltpu.roll(normal_face[s], 1, 1), 0.0) for s in range(2)]
    span_face = [spf_send[s : s + 1, :] for s in range(2)]
    spf_halo.wait_recv()
    span_left = [spl_recv[s : s + 1, :] for s in range(2)]
    diag = [
        pse_ref[s : s + 1, :] + span_left[s] + span_face[s] + normal_left[s] + normal_face[s]
        for s in range(2)
    ]

    lane64 = iota((64, 128), 1)
    first_line = ((lane64 // 32) % 2) == 0
    low_half = lane64 < 64
    perm2 = jnp.concatenate([perm, perm], axis=1)
    perm3 = jnp.concatenate([perm, perm, perm], axis=1)
    h_rows = jnp.concatenate([part(16, r, s) for s in range(2) for l in range(2) for r in range(4)], axis=0)
    c_rows = jnp.concatenate(
        [
            jnp.broadcast_to((diag, face)[q][s], (16, 128))
            for s in range(2)
            for l in range(2)
            for q in range(2)
        ],
        axis=0,
    )
    e_flat = e_send.reshape(64 * 8, 128)
    by_slot = dot(perm2, jnp.concatenate(split(h_rows), axis=1), 1, 1)
    e_flat[pl.ds(0, 64, stride=8), :] = jnp.where(first_line, by_slot[:64], by_slot[64:])
    by_slot = dot(perm3, jnp.concatenate(split3(c_rows), axis=1), 1, 1)
    e_flat[pl.ds(1, 64, stride=8), :] = jnp.where(first_line, by_slot[:64], by_slot[64:])

    def send_all(src, dst, rows, send_sem, recv_sem):
        def one(i, carry):
            peer = lax.rem(me + i, count)
            pltpu.make_async_remote_copy(
                src.at[peer, pl.ds(0, rows)],
                dst.at[me, pl.ds(0, rows)],
                send_sem,
                recv_sem,
                device_id={"stream": peer},
                device_id_type=MESH,
            ).start()
            return carry

        lax.fori_loop(1, count, one, 0)

    def wait_all(buf, rows, sem):
        blocks = buf.at[pl.ds(0, 63), pl.ds(0, rows)]
        pltpu.make_async_copy(blocks, blocks, sem).wait()

    send_all(e_send, e_recv, 2, e_sems.at[0], e_sems.at[1])
    e_recv[me] = e_send[me]

    weights_t = jnp.concatenate(
        [basis, dot3(cs_ref[...], basis, 0, 0), dot3(cn_ref[...], basis, 0, 0), side_p, jnp.zeros((8, 128), F32)],
        axis=0,
    )
    weights = jnp.transpose(weights_t)[:80]
    weights_high, weights_low = split(weights)
    weights_both = jnp.concatenate([weights_high, weights_low], axis=0)
    for load in loads_f:
        load.wait()
    for halo in m2_halos:
        halo.wait_recv()
    face_left = [masked(m2l_recv[32:33, :], 2 * me - 1), face[0]]

    for c in range(2):
        halos[2 * c].wait_recv()
        halos[2 * c + 1].wait_recv()
        columns = []
        for r in (2 * c, 2 * c + 1):
            for s in range(2):
                rs = 2 * r + s
                u = u_buf[rs]
                before = m2l_recv[8 * r : 8 * r + 8, :] if s == 0 else part(8, r, 0)
                after = part(8, r, 1) if s == 0 else m2r_recv[8 * r : 8 * r + 8, :]
                columns.append(
                    jnp.concatenate(
                        [
                            f_buf[rs],
                            span_left[s] * ul_buf[rs] + span_face[s] * ur_buf[rs],
                            normal_left[s] * pltpu.roll(u, 1, 1) + normal_face[s] * pltpu.roll(u, 127, 1),
                            (face_left[s] + face[s]) * part(0, r, s) - face_left[s] * before - face[s] * after,
                            jnp.zeros((8, 128), F32),
                        ],
                        axis=0,
                    )
                )
        high, low = split(jnp.concatenate(columns, axis=1))
        both = dot(weights_both, high)
        modal = both[:80] + (both[80:] + dot(weights_high, low))
        modal_high, modal_low = split(modal)
        g_flat = g_send.at[c].reshape(64 * 8, 128)
        for kg in range(5):
            rows = [
                jnp.concatenate(
                    [
                        half[kg * 16 : kg * 16 + 16, (2 * r + s) * 128 : (2 * r + s) * 128 + 128]
                        for s in range(2)
                        for l in range(2)
                        for r in range(2)
                    ],
                    axis=0,
                )
                for half in (modal_high, modal_low)
            ]
            by_slot = dot(perm2, jnp.concatenate(rows, axis=1), 1, 1)
            g_flat[pl.ds(kg, 64, stride=8), :] = jnp.where(first_line, by_slot[:64], by_slot[64:])
        send_all(g_send.at[c], g_recv.at[c], 5, gs_sem.at[c], gr_sem.at[c])
        g_recv[c, me] = g_send[c, me]

    lam_groups = jnp.where((iota((8, 128), 1) // 16) == row8, lam_row, 0.0)
    spread = jnp.where((row % 16) == (lane % 16), 1.0, 0.0).astype(BF16)
    lam_h, lam_m, lam_l = split3(lam_groups)
    rate = dot(lam_h, spread) + dot(lam_m, spread) + dot(lam_l, spread)
    rate_abs = jnp.abs(rate)
    wait_all(e_recv, 2, e_sems.at[1])
    e_got = e_recv.reshape(64 * 8, 128)
    coeffs = e_got[pl.ds(1, 64, stride=8), :]
    even_group = ((lane64 // 16) % 2) == 0
    d_both = jnp.where(even_group, coeffs, pltpu.roll(coeffs, 16, 1))
    f_both = jnp.where(even_group, pltpu.roll(coeffs, 112, 1), coeffs)
    f_swap = pltpu.roll(f_both, 64, 1)
    da_buf[...] = d_both
    db_buf[...] = pltpu.roll(d_both, 64, 1)
    f0_buf[...] = jnp.where(low_half, f_both, f_swap)
    f1_buf[0:8, :] = jnp.zeros((8, 128), F32)
    f1_buf[pl.ds(8, 64), :] = jnp.where(low_half, f_swap, f_both)
    low1 = lane1 < 64
    low8 = iota((8, 128), 1) < 64

    def factor_step(t, d_row, f_now, f_next, inv_before):
        x = rate * f_now
        main = d_row + rate_abs * (f_now + f_next)
        inv = 1.0 / (main - x * x * inv_before)
        inv_buf[t] = inv
        a_buf[t] = x * inv
        b_buf[t] = rate * f_next * inv
        return inv

    def factor(p, inv):
        q = 63 - p
        f_0 = jnp.where(low1, f1_buf[pl.ds(p + 7, 1), :], f1_buf[pl.ds(q + 8, 1), :])
        f_1 = jnp.where(low1, f0_buf[pl.ds(p, 1), :], f0_buf[pl.ds(q, 1), :])
        f_2 = jnp.where(low1, f1_buf[pl.ds(p + 8, 1), :], f1_buf[pl.ds(q + 7, 1), :])
        d_0 = jnp.where(low1, da_buf[pl.ds(p, 1), :], da_buf[pl.ds(q, 1), :])
        d_1 = jnp.where(low1, db_buf[pl.ds(p, 1), :], db_buf[pl.ds(q, 1), :])
        inv = factor_step(2 * p, d_0, f_0, f_1, inv)
        return factor_step(2 * p + 1, d_1, f_1, f_2, inv)

    lax.fori_loop(0, 32, factor, jnp.zeros((8, 128), F32))
    b_last = b_buf[63]
    middle = 1.0 / (1.0 - b_last * pltpu.roll(b_last, 64, 1))

    def turned(rows):
        high = rows.astype(BF16).astype(F32)
        return jnp.transpose(jnp.concatenate([high, rows - high], axis=0)).astype(BF16)

    owner = row - 64 * pair_line
    to_cell = jnp.concatenate(
        [jnp.where(lane == 2 * owner + s, 1.0, 0.0).astype(BF16) for s in range(2)], axis=0
    )
    to_normal = jnp.concatenate([perm[:64], perm[:64], perm[64:], perm[64:]], axis=0)
    h_turned = turned(e_got[pl.ds(0, 64, stride=8), :])
    h_own = dot(jnp.concatenate([h_turned[:64], h_turned[64:]], axis=1), to_cell)
    basis_88 = basis_z[:, 0:88]
    basis_high, basis_low = split(basis_88)
    basis_both = jnp.concatenate([basis_high, basis_low], axis=0)

    def leave_modes(flat, select, lines, side_rows):
        pieces = []
        for kg in range(5):
            t = turned(flat[pl.ds(kg, 64, stride=8), :])
            if lines:
                pair = (jnp.concatenate([t[0:32], t[64:96]], axis=0), jnp.concatenate([t[32:64], t[96:128]], axis=0))
            else:
                pair = (t[:64], t[64:])
            pieces.append(jnp.concatenate(pair, axis=1))
        moved = dot(jnp.concatenate(pieces, axis=0), select)
        columns = [
            jnp.concatenate(
                [moved[kg * 64 + x * 32 + r * 16 : kg * 64 + x * 32 + r * 16 + 16] for kg in range(5)]
                + [side_rows(x, r)],
                axis=0,
            )
            for r in range(2)
            for x in range(2)
        ]
        high, low = split(jnp.concatenate(columns, axis=1))
        both = dot(basis_both, high)
        return both[:80] + (both[80:] + dot(basis_high, low))

    stores = []
    for c in range(2):
        wait_all(g_recv.at[c], 5, gr_sem.at[c])

        def forward(p, d, c=c):
            near = g_recv[c, p]
            far = g_recv[c, 63 - p]
            d = inv_buf[2 * p] * jnp.where(low8, near, far) + a_buf[2 * p] * d
            d_buf[2 * p] = d
            odd = pltpu.roll(jnp.where(low8, far, near), 64, 1)
            d = inv_buf[2 * p + 1] * odd + a_buf[2 * p + 1] * d
            d_buf[2 * p + 1] = d
            return d

        d = lax.fori_loop(0, 32, forward, jnp.zeros((8, 128), F32))
        y = (d + b_last * pltpu.roll(d, 64, 1)) * middle

        def backward(i, y, c=c):
            p = 31 - i
            y_odd = d_buf[2 * p + 1] + b_buf[2 * p + 1] * y
            y_even = d_buf[2 * p] + b_buf[2 * p] * y_odd
            swapped = pltpu.roll(y_odd, 64, 1)
            y_send[c, p] = jnp.where(low8, y_even, swapped)
            y_send[c, 63 - p] = jnp.where(low8, swapped, y_even)
            return y_even

        lax.fori_loop(0, 32, backward, pltpu.roll(y, 64, 1))
        send_all(y_send.at[c], y_recv.at[c], 5, ys_sem.at[c], yr_sem.at[c])
        y_recv[c, me] = y_send[c, me]
        left = leave_modes(
            y_send.at[c].reshape(64 * 8, 128),
            to_cell,
            False,
            lambda x, r, c=c: h_own[x * 32 + (2 * c + r) * 8 : x * 32 + (2 * c + r) * 8 + 8],
        )
        for r in range(2):
            for x in range(2):
                at = (2 * c + r) * 2 + x
                ls_buf[at] = left[:, (2 * r + x) * 128 : (2 * r + x) * 128 + 128]
                stores.append(
                    pltpu.make_async_copy(ls_buf.at[at], out_ls.at[:, 2 * c + r, x, 0, :], out_sem.at[at])
                )
                stores[-1].start()
    for c in range(2):
        wait_all(y_recv.at[c], 5, yr_sem.at[c])
        left = leave_modes(
            y_recv.at[c].reshape(64 * 8, 128), to_normal, True, lambda x, r, c=c: part(16, 2 * c + r, x)
        )
        for r in range(2):
            for x in range(2):
                at = (2 * c + r) * 2 + x
                rel_buf[at] = left[:, (2 * r + x) * 128 : (2 * r + x) * 128 + 128]
                stores.append(
                    pltpu.make_async_copy(rel_buf.at[at], out_rel.at[:, 2 * c + r, x, 0, :], out_sem.at[8 + at])
                )
                stores[-1].start()

    spf_halo.wait_send()
    for halo in m2_halos:
        halo.wait_send()
    for halo in halos:
        halo.wait_send()
    wait_all(e_send, 2, e_sems.at[0])
    for c in range(2):
        wait_all(g_send.at[c], 5, gs_sem.at[c])
        wait_all(y_send.at[c], 5, ys_sem.at[c])
    for store in stores:
        store.wait()


def per_device(
    solution, forcing, pseudo_shift, stream_faces, span_faces, normal_faces, coupling_span, coupling_normal,
    reflectors, eigenvalues, line_start, line_length, line_order,
):
    hbm = pl.BlockSpec(memory_space=pltpu.HBM)
    block = pltpu.VMEM((8, 80, 128), F32)
    per_peer = pltpu.VMEM((64, 8, 128), F32)
    pair_per_peer = pltpu.VMEM((2, 64, 8, 128), F32)
    two = pltpu.VMEM((2, 128), F32)
    line = pltpu.VMEM((1, 128), jnp.int32)
    dma = pltpu.SemaphoreType.DMA
    out = jax.ShapeDtypeStruct((80, 4, 2, 1, 128), F32)
    relaxed, line_states = pl.pallas_call(
        body,
        out_shape=(out, out),
        in_specs=[hbm] * 13,
        out_specs=(hbm, hbm),
        scratch_shapes=[
            two, two, two, pltpu.VMEM((80, 80), F32), pltpu.VMEM((80, 80), F32),
            pltpu.VMEM((8, 80), F32), pltpu.VMEM((1, 80), F32), line, line, line,
            block, block, block, block,
            two, two,
            pltpu.VMEM((2, 40, 128), F32), pltpu.VMEM((40, 128), F32), pltpu.VMEM((40, 128), F32),
            per_peer, per_peer, pair_per_peer, pair_per_peer, pair_per_peer, pair_per_peer,
            pltpu.VMEM((16, 128), F32),
            pltpu.VMEM((64, 128), F32), pltpu.VMEM((64, 128), F32), pltpu.VMEM((64, 128), F32), pltpu.VMEM((72, 128), F32),
            per_peer, per_peer, per_peer, per_peer, block, block,
            dma((27,)), dma((16,)), dma((4,)), dma((4,)), dma((3,)), dma((3,)),
            dma((2,)), dma((2,)), dma((2,)), dma((2,)), dma((2,)),
        ],
        compiler_params=pltpu.CompilerParams(
            collective_id=0, has_side_effects=True, vmem_limit_bytes=63 << 20
        ),
        name="relax",
    )(
        solution, forcing, pseudo_shift, stream_faces, span_faces, normal_faces,
        coupling_span, coupling_normal, reflectors, eigenvalues.reshape(1, 80), line_start, line_length, line_order,
    )
    return relaxed, line_states.reshape(80, 4, 2, 128)


def solution(mesh):
    cells = P(None, None, "stream", "span", None)
    weights = P("stream", "span", None)
    tiles = P("span", None)
    return jax.shard_map(
        per_device,
        mesh=mesh,
        in_specs=(cells, cells, weights, weights, weights, weights, P(), P(), P(), P(), tiles, tiles, tiles),
        out_specs=(cells, P(None, None, ("span", "stream"), None)),
        check_vma=False,
    )
```

```python
import functools

import jax
import jax.numpy as jnp
from jax import lax
from jax.experimental import pallas as pl
from jax.experimental.pallas import tpu as pltpu
from jax.sharding import PartitionSpec as P

F32 = jnp.float32
BF16 = jnp.bfloat16
MESH = pl.DeviceIdType.MESH
EPS = 1e-06


def iota(shape, dim):
    return lax.broadcasted_iota(jnp.int32, shape, dim)


def split(x):
    high = x.astype(BF16)
    return high, (x - high.astype(F32)).astype(BF16)


def split3(x):
    high = x.astype(BF16)
    rest = x - high.astype(F32)
    mid = rest.astype(BF16)
    return high, mid, (rest - mid.astype(F32)).astype(BF16)


def dot(a, b, ca=1, cb=0):
    return lax.dot_general(a, b, (((ca,), (cb,)), ((), ())), preferred_element_type=F32)


def dot3(a, b, ca=1, cb=0):
    ah, al = split(a)
    bh, bl = split(b)
    return dot(ah, bh, ca, cb) + (dot(al, bh, ca, cb) + dot(ah, bl, ca, cb))


def body(
    sol, frc, pse, stf, spf, nof, cs, cn, reflectors, lam, start, length, order,
    out_rel, out_ls,
    pse_ref, stf_ref, nof_ref, cs_ref, cn_ref, refl_ref, lam_ref, start_ref, length_ref, order_ref,
    u_buf, ul_buf, ur_buf, f_buf, spf_send, spl_recv, m2_send, m2l_recv, m2r_recv,
    e_send, e_recv, g_send, g_recv, y_send, y_recv,
    pad_buf, da_buf, db_buf, f0_buf, f1_buf, inv_buf, a_buf, b_buf, d_buf, modal_buf,
    loc_sem, halo_send_sem, halo_recv_sem, tiny_send_sem, tiny_recv_sem,
    e_sems, gs_sem, gr_sem, ys_sem, yr_sem,
):
    me = lax.axis_index("stream")
    count = lax.axis_size("stream")
    sp = lax.axis_index("span")
    sp_count = lax.axis_size("span")
    sp_left = lax.rem(sp + sp_count - 1, sp_count)
    sp_right = lax.rem(sp + 1, sp_count)
    st_left = lax.rem(me + count - 1, count)
    st_right = lax.rem(me + 1, count)

    def peer_of(i):
        return lax.rem(me + 1 + lax.rem(i + 26, count - 1), count)

    g_recv[...] = jnp.zeros_like(g_recv)
    barrier = pltpu.get_barrier_semaphore()
    for side in (sp_left, sp_right):
        pl.semaphore_signal(barrier, inc=1, device_id={"span": side}, device_id_type=MESH)

    def greet(i, carry):
        pl.semaphore_signal(
            barrier, inc=1, device_id={"stream": peer_of(i)}, device_id_type=MESH
        )
        return carry

    lax.fori_loop(0, count - 1, greet, 0)

    loads_u = [
        pltpu.make_async_copy(sol.at[:, rs // 2, rs % 2, 0, :], u_buf.at[rs], loc_sem.at[rs]) for rs in range(8)
    ]
    loads_f = [
        pltpu.make_async_copy(frc.at[:, rs // 2, rs % 2, 0, :], f_buf.at[rs], loc_sem.at[8 + rs]) for rs in range(8)
    ]
    first = ((order, order_ref), (spf.at[:, 0], spf_send), (reflectors, refl_ref), (lam, lam_ref))
    later = (
        (cs, cs_ref), (cn, cn_ref), (pse.at[:, 0], pse_ref), (stf.at[:, 0], stf_ref), (nof.at[:, 0], nof_ref),
        (start, start_ref), (length, length_ref),
    )
    loads_small = [
        pltpu.make_async_copy(src, dst, loc_sem.at[16 + i]) for i, (src, dst) in enumerate(first + later)
    ]
    for load in loads_small[:4]:
        load.start()
    for load in loads_u:
        load.start()
    for load in loads_small[4:]:
        load.start()
    for load in loads_f:
        load.start()


    for load in loads_small[:4]:
        load.wait()

    lane = iota((128, 128), 1)
    row = iota((128, 128), 0)
    perm_t = jnp.where(row == order_ref[...], 1.0, 0.0).astype(BF16)
    pair_line = row // 64
    pick = jnp.where(lane == 2 * (row - 64 * pair_line) + pair_line, 1.0, 0.0).astype(BF16)
    perm = dot(pick, perm_t, 1, 1).astype(BF16)

    for load in loads_small[4:]:
        load.wait()

    pad_buf[...] = jnp.zeros_like(pad_buf)
    pad_buf[0:8, 0:80] = refl_ref[...]
    pad_buf[8:9, 0:80] = lam_ref[...]
    refl = pad_buf[0:8, :]
    lam_row = pad_buf[8:9, :]
    norms = jnp.sum(refl * refl, axis=1, keepdims=True)
    factors = 2.0 / (norms + EPS)
    scales = 2.0 * (EPS**0.5) / (norms + EPS)
    lane80 = iota((80, 128), 1)
    row8 = iota((8, 128), 0)
    basis = jnp.where(iota((80, 128), 0) == lane80, 1.0, 0.0)
    side_z = jnp.zeros((80, 128), F32)
    side_p = jnp.zeros((8, 128), F32)
    for k in range(8):
        w = refl[k : k + 1, :]
        factor = factors[k : k + 1, :]
        z = jnp.sum(basis * w, axis=1, keepdims=True)
        basis = basis - (factor * z) * w
        side_z = jnp.where(lane80 == 80 + k, z * scales[k : k + 1, :], side_z)
        side_p = side_p - (factor * jnp.sum(side_p * w, axis=1, keepdims=True)) * w
        side_p = jnp.where(row8 == k, w, side_p)
    side_p = side_p * scales
    basis_z = basis + side_z
    zt = jnp.transpose(jnp.concatenate([basis_z, jnp.zeros((48, 128), F32)], axis=0))[80:88, 0:80]
    m1 = dot3(side_p * jnp.abs(lam_row), basis, 1, 1)
    m2 = dot3(side_p * lam_row, basis, 1, 1)
    small = jnp.concatenate([m1, m2, zt], axis=0)
    for load in loads_u:
        load.wait()
    state = jnp.concatenate([u_buf[rs] for rs in range(8)], axis=1)
    small_u = dot3(small, state)

    def part(base, r, s):
        rs = 2 * r + s
        return small_u[base : base + 8, rs * 128 : rs * 128 + 128]

    for s in range(2):
        for r in range(4):
            m2_send[s, 8 * r : 8 * r + 8, :] = part(8, r, s)
        m2_send[s, 32:40, :] = jnp.broadcast_to(stf_ref[s : s + 1, :], (8, 128))
    line_start = start_ref[...]
    line_end = line_start + length_ref[...]

    def masked(faces, pos):
        return jnp.where((pos >= line_start) & (pos + 1 < line_end), faces, 0.0)

    face = [masked(stf_ref[s : s + 1, :], 2 * me + s) for s in range(2)]
    lane1 = iota((1, 128), 1)
    normal_face = [jnp.where(lane1 < 127, nof_ref[s : s + 1, :], 0.0) for s in range(2)]
    normal_left = [jnp.where(lane1 > 0, pltpu.roll(normal_face[s], 1, 1), 0.0) for s in range(2)]
    span_face = [spf_send[s : s + 1, :] for s in range(2)]
    local_t = jnp.concatenate([basis, dot3(cn_ref[...], basis, 0, 0)], axis=0)
    outer_t = jnp.concatenate([dot3(cs_ref[...], basis, 0, 0), side_p, jnp.zeros((8, 128), F32)], axis=0)
    pad_rows = jnp.zeros((32, 128), F32)
    turned_t = jnp.transpose(jnp.concatenate([local_t, outer_t], axis=0))[:80]
    local_weights = split(turned_t[:, 0:160])
    outer_weights = split(jnp.transpose(jnp.concatenate([outer_t, pad_rows], axis=0))[:80, 0:96])

    def apply(pair, rows):
        high, low = split(rows)
        both = dot(jnp.concatenate(pair, axis=0), high)
        return both[:80] + (both[80:] + dot(pair[0], low))

    for load in loads_f:
        load.wait()
    for c in range(2):
        columns = []
        for rs in range(4 * c, 4 * c + 4):
            s = rs % 2
            u = u_buf[rs]
            columns.append(
                jnp.concatenate(
                    [
                        f_buf[rs],
                        normal_left[s] * pltpu.roll(u, 1, 1) + normal_face[s] * pltpu.roll(u, 127, 1),
                    ],
                    axis=0,
                )
            )
        modal_buf[c] = apply(local_weights, jnp.concatenate(columns, axis=1))

    pl.semaphore_wait(barrier, count + 1)

    halos = []
    for c in range(2):
        for k, (side, buf) in enumerate(((sp_right, ul_buf), (sp_left, ur_buf))):
            halo = pltpu.make_async_remote_copy(
                u_buf.at[pl.ds(4 * c, 4)],
                buf.at[pl.ds(4 * c, 4)],
                halo_send_sem.at[2 * c + k],
                halo_recv_sem.at[2 * c + k],
                device_id={"span": side},
                device_id_type=MESH,
            )
            if c == 0 and k == 0:
                spf_halo = pltpu.make_async_remote_copy(
                    spf_send, spl_recv, tiny_send_sem.at[0], tiny_recv_sem.at[0],
                    device_id={"span": sp_right}, device_id_type=MESH,
                )
                spf_halo.start()
            halo.start()
            halos.append(halo)

    m2_halos = [
        pltpu.make_async_remote_copy(
            m2_send.at[1 - k], buf, tiny_send_sem.at[1 + k], tiny_recv_sem.at[1 + k],
            device_id={"stream": side}, device_id_type=MESH,
        )
        for k, (side, buf) in enumerate(((st_right, m2l_recv), (st_left, m2r_recv)))
    ]
    for halo in m2_halos:
        halo.start()

    spf_halo.wait_recv()
    span_left = [spl_recv[s : s + 1, :] for s in range(2)]
    diag = [
        pse_ref[s : s + 1, :] + span_left[s] + span_face[s] + normal_left[s] + normal_face[s]
        for s in range(2)
    ]

    lane64 = iota((64, 128), 1)
    first_line = ((lane64 // 32) % 2) == 0
    low_half = lane64 < 64
    perm2 = jnp.concatenate([perm, perm], axis=1)
    perm3 = jnp.concatenate([perm, perm, perm], axis=1)
    h_rows = jnp.concatenate([part(16, r, s) for s in range(2) for l in range(2) for r in range(4)], axis=0)
    c_rows = jnp.concatenate(
        [
            jnp.broadcast_to((diag, face)[q][s], (16, 128))
            for s in range(2)
            for l in range(2)
            for q in range(2)
        ],
        axis=0,
    )
    e_flat = e_send.reshape(64 * 8, 128)
    by_slot = dot(perm2, jnp.concatenate(split(h_rows), axis=1), 1, 1)
    e_flat[pl.ds(0, 64, stride=8), :] = jnp.where(first_line, by_slot[:64], by_slot[64:])
    by_slot = dot(perm3, jnp.concatenate(split3(c_rows), axis=1), 1, 1)
    e_flat[pl.ds(1, 64, stride=8), :] = jnp.where(first_line, by_slot[:64], by_slot[64:])

    def send_all(src, dst, rows, send_sem, recv_sem):
        def one(i, carry):
            peer = lax.rem(me + 1 + lax.rem(i * 26 + 26, count - 1), count)
            pltpu.make_async_remote_copy(
                src.at[peer, pl.ds(0, rows)],
                dst.at[me, pl.ds(0, rows)],
                send_sem,
                recv_sem,
                device_id={"stream": peer},
                device_id_type=MESH,
            ).start()
            return carry

        lax.fori_loop(0, count - 1, one, 0)

    def wait_all(buf, rows, sem):
        blocks = buf.at[pl.ds(0, 63), pl.ds(0, rows)]
        pltpu.make_async_copy(blocks, blocks, sem).wait()

    send_all(e_send, e_recv, 2, e_sems.at[0], e_sems.at[1])
    e_recv[me] = e_send[me]

    for halo in m2_halos:
        halo.wait_recv()
    face_left = [masked(m2l_recv[32:33, :], 2 * me - 1), face[0]]

    for c in range(2):
        halos[2 * c].wait_recv()
        halos[2 * c + 1].wait_recv()
        columns = []
        for r in (2 * c, 2 * c + 1):
            for s in range(2):
                rs = 2 * r + s
                before = m2l_recv[8 * r : 8 * r + 8, :] if s == 0 else part(8, r, 0)
                after = part(8, r, 1) if s == 0 else m2r_recv[8 * r : 8 * r + 8, :]
                columns.append(
                    jnp.concatenate(
                        [
                            span_left[s] * ul_buf[rs] + span_face[s] * ur_buf[rs],
                            (face_left[s] + face[s]) * part(0, r, s) - face_left[s] * before - face[s] * after,
                            jnp.zeros((8, 128), F32),
                        ],
                        axis=0,
                    )
                )
        modal = modal_buf[c] + apply(outer_weights, jnp.concatenate(columns, axis=1))
        modal_high, modal_low = split(modal)
        g_flat = g_send.at[c].reshape(64 * 8, 128)
        for kg in range(5):
            rows = [
                jnp.concatenate(
                    [
                        half[kg * 16 : kg * 16 + 16, (2 * r + s) * 128 : (2 * r + s) * 128 + 128]
                        for s in range(2)
                        for l in range(2)
                        for r in range(2)
                    ],
                    axis=0,
                )
                for half in (modal_high, modal_low)
            ]
            by_slot = dot(perm2, jnp.concatenate(rows, axis=1), 1, 1)
            g_flat[pl.ds(kg, 64, stride=8), :] = jnp.where(first_line, by_slot[:64], by_slot[64:])
        send_all(g_send.at[c], g_recv.at[c], 5, gs_sem.at[c], gr_sem.at[c])
        g_recv[c, me] = g_send[c, me]

    lam_groups = jnp.where((iota((8, 128), 1) // 16) == row8, lam_row, 0.0)
    spread = jnp.where((row % 16) == (lane % 16), 1.0, 0.0).astype(BF16)
    lam_h, lam_m, lam_l = split3(lam_groups)
    rate = dot(lam_h, spread) + dot(lam_m, spread) + dot(lam_l, spread)
    rate_abs = jnp.abs(rate)
    wait_all(e_recv, 2, e_sems.at[1])
    e_got = e_recv.reshape(64 * 8, 128)
    coeffs = e_got[pl.ds(1, 64, stride=8), :]
    even_group = ((lane64 // 16) % 2) == 0
    d_both = jnp.where(even_group, coeffs, pltpu.roll(coeffs, 16, 1))
    f_both = jnp.where(even_group, pltpu.roll(coeffs, 112, 1), coeffs)
    f_swap = pltpu.roll(f_both, 64, 1)
    da_buf[...] = d_both
    db_buf[...] = pltpu.roll(d_both, 64, 1)
    f0_buf[...] = jnp.where(low_half, f_both, f_swap)
    f1_buf[0:8, :] = jnp.zeros((8, 128), F32)
    f1_buf[pl.ds(8, 64), :] = jnp.where(low_half, f_swap, f_both)
    low1 = lane1 < 64
    low8 = iota((8, 128), 1) < 64

    def factor_step(t, d_row, f_now, f_next, inv_before):
        x = rate * f_now
        main = d_row + rate_abs * (f_now + f_next)
        inv = 1.0 / (main - x * x * inv_before)
        inv_buf[t] = inv
        a_buf[t] = x * inv
        b_buf[t] = rate * f_next * inv
        return inv

    def factor(p, inv):
        q = 63 - p
        f_0 = jnp.where(low1, f1_buf[pl.ds(p + 7, 1), :], f1_buf[pl.ds(q + 8, 1), :])
        f_1 = jnp.where(low1, f0_buf[pl.ds(p, 1), :], f0_buf[pl.ds(q, 1), :])
        f_2 = jnp.where(low1, f1_buf[pl.ds(p + 8, 1), :], f1_buf[pl.ds(q + 7, 1), :])
        d_0 = jnp.where(low1, da_buf[pl.ds(p, 1), :], da_buf[pl.ds(q, 1), :])
        d_1 = jnp.where(low1, db_buf[pl.ds(p, 1), :], db_buf[pl.ds(q, 1), :])
        inv = factor_step(2 * p, d_0, f_0, f_1, inv)
        return factor_step(2 * p + 1, d_1, f_1, f_2, inv)

    lax.fori_loop(0, 32, factor, jnp.zeros((8, 128), F32))
    b_last = b_buf[63]
    middle = 1.0 / (1.0 - b_last * pltpu.roll(b_last, 64, 1))

    def turned(rows):
        high = rows.astype(BF16).astype(F32)
        return jnp.transpose(jnp.concatenate([high, rows - high], axis=0)).astype(BF16)

    owner = row - 64 * pair_line
    to_cell = jnp.concatenate(
        [jnp.where(lane == 2 * owner + s, 1.0, 0.0).astype(BF16) for s in range(2)], axis=0
    )
    to_normal = jnp.concatenate([perm[:64], perm[:64], perm[64:], perm[64:]], axis=0)
    h_turned = turned(e_got[pl.ds(0, 64, stride=8), :])
    h_own = dot(jnp.concatenate([h_turned[:64], h_turned[64:]], axis=1), to_cell)
    basis_88 = basis_z[:, 0:88]
    basis_high, basis_low = split(basis_88)
    basis_both = jnp.concatenate([basis_high, basis_low], axis=0)

    def leave_modes(flat, select, lines, side_rows):
        pieces = []
        for kg in range(5):
            t = turned(flat[pl.ds(kg, 64, stride=8), :])
            if lines:
                pair = (jnp.concatenate([t[0:32], t[64:96]], axis=0), jnp.concatenate([t[32:64], t[96:128]], axis=0))
            else:
                pair = (t[:64], t[64:])
            pieces.append(jnp.concatenate(pair, axis=1))
        moved = dot(jnp.concatenate(pieces, axis=0), select)
        columns = [
            jnp.concatenate(
                [moved[kg * 64 + x * 32 + r * 16 : kg * 64 + x * 32 + r * 16 + 16] for kg in range(5)]
                + [side_rows(x, r)],
                axis=0,
            )
            for r in range(2)
            for x in range(2)
        ]
        high, low = split(jnp.concatenate(columns, axis=1))
        both = dot(basis_both, high)
        return both[:80] + (both[80:] + dot(basis_high, low))

    for c in range(2):
        wait_all(g_recv.at[c], 5, gr_sem.at[c])

        d = None
        for p in range(32):
            near = g_recv[c, p]
            far = g_recv[c, 63 - p]
            even = inv_buf[2 * p] * jnp.where(low8, near, far)
            d = even if d is None else even + a_buf[2 * p] * d
            d_buf[2 * p] = d
            odd = pltpu.roll(jnp.where(low8, far, near), 64, 1)
            d = inv_buf[2 * p + 1] * odd + a_buf[2 * p + 1] * d
            d_buf[2 * p + 1] = d
        y = pltpu.roll((d + b_last * pltpu.roll(d, 64, 1)) * middle, 64, 1)
        for p in reversed(range(32)):
            y_odd = d_buf[2 * p + 1] + b_buf[2 * p + 1] * y
            y = d_buf[2 * p] + b_buf[2 * p] * y_odd
            swapped = pltpu.roll(y_odd, 64, 1)
            y_send[c, p] = jnp.where(low8, y, swapped)
            y_send[c, 63 - p] = jnp.where(low8, swapped, y)
        send_all(y_send.at[c], y_recv.at[c], 5, ys_sem.at[c], yr_sem.at[c])
        y_recv[c, me] = y_send[c, me]
        left = leave_modes(
            y_send.at[c].reshape(64 * 8, 128),
            to_cell,
            False,
            lambda x, r, c=c: h_own[x * 32 + (2 * c + r) * 8 : x * 32 + (2 * c + r) * 8 + 8],
        )
        for r in range(2):
            for x in range(2):
                at = (2 * c + r) * 2 + x
                out_ls[at] = left[:, (2 * r + x) * 128 : (2 * r + x) * 128 + 128]
    for c in range(2):
        wait_all(y_recv.at[c], 5, yr_sem.at[c])
        left = leave_modes(
            y_recv.at[c].reshape(64 * 8, 128), to_normal, True, lambda x, r, c=c: part(16, 2 * c + r, x)
        )
        for r in range(2):
            for x in range(2):
                at = (2 * c + r) * 2 + x
                out_rel[at] = left[:, (2 * r + x) * 128 : (2 * r + x) * 128 + 128]

    spf_halo.wait_send()
    for halo in m2_halos:
        halo.wait_send()
    for halo in halos:
        halo.wait_send()
    wait_all(e_send, 2, e_sems.at[0])
    for c in range(2):
        wait_all(g_send.at[c], 5, gs_sem.at[c])
        wait_all(y_send.at[c], 5, ys_sem.at[c])


def store(rel, lines, out_rel, out_ls, sem):
    copies = []
    for at in range(8):
        for k, (src, dst) in enumerate(((rel, out_rel), (lines, out_ls))):
            copies.append(pltpu.make_async_copy(src.at[at], dst.at[:, at // 2, at % 2, 0, :], sem.at[8 * k + at]))
    for copy in copies:
        copy.start()
    for copy in copies:
        copy.wait()


def per_device(
    solution, forcing, pseudo_shift, stream_faces, span_faces, normal_faces, coupling_span, coupling_normal,
    reflectors, eigenvalues, line_start, line_length, line_order,
):
    vmem = pl.BlockSpec(memory_space=pltpu.VMEM)
    hbm = pl.BlockSpec(memory_space=pltpu.HBM)
    block = pltpu.VMEM((8, 80, 128), F32)
    per_peer = pltpu.VMEM((64, 8, 128), F32)
    pair_per_peer = pltpu.VMEM((2, 64, 8, 128), F32)
    two = pltpu.VMEM((2, 128), F32)
    line = pltpu.VMEM((1, 128), jnp.int32)
    dma = pltpu.SemaphoreType.DMA
    out = jax.ShapeDtypeStruct((8, 80, 128), F32)
    relaxed, line_states = pl.pallas_call(
        body,
        out_shape=(out, out),
        in_specs=[hbm] * 13,
        out_specs=(vmem, vmem),
        scratch_shapes=[
            two, two, two, pltpu.VMEM((80, 80), F32), pltpu.VMEM((80, 80), F32),
            pltpu.VMEM((8, 80), F32), pltpu.VMEM((1, 80), F32), line, line, line,
            block, block, block, block,
            two, two,
            pltpu.VMEM((2, 40, 128), F32), pltpu.VMEM((40, 128), F32), pltpu.VMEM((40, 128), F32),
            per_peer, per_peer, pair_per_peer, pair_per_peer, pair_per_peer, pair_per_peer,
            pltpu.VMEM((16, 128), F32),
            pltpu.VMEM((64, 128), F32), pltpu.VMEM((64, 128), F32), pltpu.VMEM((64, 128), F32), pltpu.VMEM((72, 128), F32),
            per_peer, per_peer, per_peer, per_peer, pltpu.VMEM((2, 80, 512), F32),
            dma((27,)), dma((4,)), dma((4,)), dma((3,)), dma((3,)),
            dma((2,)), dma((2,)), dma((2,)), dma((2,)), dma((2,)),
        ],
        compiler_params=pltpu.CompilerParams(
            collective_id=0, has_side_effects=True, vmem_limit_bytes=48 << 20
        ),
        name="relax",
    )(*(pltpu.with_memory_space_constraint(a, pltpu.HBM) for a in (
        solution, forcing, pseudo_shift, stream_faces, span_faces, normal_faces,
        coupling_span, coupling_normal, reflectors, eigenvalues.reshape(1, 80), line_start, line_length, line_order,
    )))
    result = jax.ShapeDtypeStruct((80, 4, 2, 1, 128), F32)
    anywhere = pl.BlockSpec(memory_space=pl.ANY)
    relaxed, line_states = pl.pallas_call(
        store,
        out_shape=(result, result),
        in_specs=[anywhere, anywhere],
        out_specs=(hbm, hbm),
        scratch_shapes=[dma((16,))],
        compiler_params=pltpu.CompilerParams(vmem_limit_bytes=48 << 20),
        name="relaxstore",
    )(relaxed, line_states)
    return relaxed, line_states.reshape(80, 4, 2, 128)


def solution(mesh):
    cells = P(None, None, "stream", "span", None)
    weights = P("stream", "span", None)
    tiles = P("span", None)
    return jax.shard_map(
        per_device,
        mesh=mesh,
        in_specs=(cells, cells, weights, weights, weights, weights, P(), P(), P(), P(), tiles, tiles, tiles),
        out_specs=(cells, P(None, None, ("span", "stream"), None)),
        check_vma=False,
    )
```

```python
import functools

import jax
import jax.numpy as jnp
from jax import lax
from jax.experimental import pallas as pl
from jax.experimental.pallas import tpu as pltpu
from jax.sharding import PartitionSpec as P

F32 = jnp.float32
BF16 = jnp.bfloat16
MESH = pl.DeviceIdType.MESH
EPS = 1e-06


def iota(shape, dim):
    return lax.broadcasted_iota(jnp.int32, shape, dim)


def split(x):
    high = x.astype(BF16)
    return high, (x - high.astype(F32)).astype(BF16)


def split3(x):
    high = x.astype(BF16)
    rest = x - high.astype(F32)
    mid = rest.astype(BF16)
    return high, mid, (rest - mid.astype(F32)).astype(BF16)


def dot(a, b, ca=1, cb=0):
    return lax.dot_general(a, b, (((ca,), (cb,)), ((), ())), preferred_element_type=F32)


def dot3(a, b, ca=1, cb=0):
    ah, al = split(a)
    bh, bl = split(b)
    return dot(ah, bh, ca, cb) + (dot(al, bh, ca, cb) + dot(ah, bl, ca, cb))


def body(
    sol, frc, pse, stf, spf, nof, cs, cn, reflectors, lam, start, length, order,
    out_rel, out_ls,
    pse_ref, stf_ref, nof_ref, cs_ref, cn_ref, refl_ref, lam_ref, start_ref, length_ref, order_ref,
    u_buf, ul_buf, ur_buf, f_buf, spf_send, spl_recv, m2_send, m2l_recv, m2r_recv,
    e_send, e_recv, g_send, g_recv, y_send, y_recv,
    pad_buf, da_buf, db_buf, f0_buf, f1_buf, inv_buf, a_buf, b_buf, d_buf, modal_buf,
    loc_sem, halo_send_sem, halo_recv_sem, tiny_send_sem, tiny_recv_sem,
    e_sems, gs_sem, gr_sem, ys_sem, yr_sem,
):
    me = lax.axis_index("stream")
    count = lax.axis_size("stream")
    sp = lax.axis_index("span")
    sp_count = lax.axis_size("span")
    sp_left = lax.rem(sp + sp_count - 1, sp_count)
    sp_right = lax.rem(sp + 1, sp_count)
    st_left = lax.rem(me + count - 1, count)
    st_right = lax.rem(me + 1, count)


    def peer_of(i):
        jz, jy = i // 8, lax.rem(i, 8)
        dy = 8 + (4 + ((jy + 1) // 2) * (1 - 2 * lax.rem(jy, 2)))
        dz = 8 + (4 + ((jz + 1) // 2) * (1 - 2 * lax.rem(jz, 2)))
        return lax.rem(me // 8 + dy, 8) * 8 + lax.rem(lax.rem(me, 8) + dz, 8)

    g_recv[...] = jnp.zeros_like(g_recv)
    barrier = pltpu.get_barrier_semaphore()
    for side in (sp_left, sp_right):
        pl.semaphore_signal(barrier, inc=1, device_id={"span": side}, device_id_type=MESH)

    def greet(i, carry):
        pl.semaphore_signal(
            barrier, inc=1, device_id={"stream": peer_of(i)}, device_id_type=MESH
        )
        return carry

    lax.fori_loop(0, count - 1, greet, 0, unroll=9)

    loads_u = [
        pltpu.make_async_copy(sol.at[:, rs // 2, rs % 2, 0, :], u_buf.at[rs], loc_sem.at[rs]) for rs in range(8)
    ]
    loads_f = [
        pltpu.make_async_copy(frc.at[:, rs // 2, rs % 2, 0, :], f_buf.at[rs], loc_sem.at[8 + rs]) for rs in range(8)
    ]
    first = ((order, order_ref), (spf.at[:, 0], spf_send), (reflectors, refl_ref), (lam, lam_ref))
    later = (
        (cs, cs_ref), (cn, cn_ref), (pse.at[:, 0], pse_ref), (stf.at[:, 0], stf_ref), (nof.at[:, 0], nof_ref),
        (start, start_ref), (length, length_ref),
    )
    loads_small = [
        pltpu.make_async_copy(src, dst, loc_sem.at[16 + i]) for i, (src, dst) in enumerate(first + later)
    ]
    for load in loads_small[:4]:
        load.start()
    for load in loads_u:
        load.start()
    for load in loads_small[4:]:
        load.start()
    for load in loads_f:
        load.start()


    for load in loads_small[:4]:
        load.wait()

    lane = iota((128, 128), 1)
    row = iota((128, 128), 0)
    perm_t = jnp.where(row == order_ref[...], 1.0, 0.0).astype(BF16)
    pair_line = row // 64
    pick = jnp.where(lane == 2 * (row - 64 * pair_line) + pair_line, 1.0, 0.0).astype(BF16)
    perm = dot(pick, perm_t, 1, 1).astype(BF16)

    for load in loads_small[4:]:
        load.wait()

    pad_buf[...] = jnp.zeros_like(pad_buf)
    pad_buf[0:8, 0:80] = refl_ref[...]
    pad_buf[8:9, 0:80] = lam_ref[...]
    refl = pad_buf[0:8, :]
    lam_row = pad_buf[8:9, :]
    norms = jnp.sum(refl * refl, axis=1, keepdims=True)
    factors = 2.0 / (norms + EPS)
    scales = 2.0 * (EPS**0.5) / (norms + EPS)
    lane80 = iota((80, 128), 1)
    row8 = iota((8, 128), 0)
    basis = jnp.where(iota((80, 128), 0) == lane80, 1.0, 0.0)
    side_z = jnp.zeros((80, 128), F32)
    side_p = jnp.zeros((8, 128), F32)
    for k in range(8):
        w = refl[k : k + 1, :]
        factor = factors[k : k + 1, :]
        z = jnp.sum(basis * w, axis=1, keepdims=True)
        basis = basis - (factor * z) * w
        side_z = jnp.where(lane80 == 80 + k, z * scales[k : k + 1, :], side_z)
        side_p = side_p - (factor * jnp.sum(side_p * w, axis=1, keepdims=True)) * w
        side_p = jnp.where(row8 == k, w, side_p)
    side_p = side_p * scales
    basis_z = basis + side_z
    zt = jnp.transpose(jnp.concatenate([basis_z, jnp.zeros((48, 128), F32)], axis=0))[80:88, 0:80]
    m1 = dot3(side_p * jnp.abs(lam_row), basis, 1, 1)
    m2 = dot3(side_p * lam_row, basis, 1, 1)
    small = jnp.concatenate([m1, m2, zt], axis=0)
    for load in loads_u:
        load.wait()
    state = jnp.concatenate([u_buf[rs] for rs in range(8)], axis=1)
    small_u = dot3(small, state)

    def part(base, r, s):
        rs = 2 * r + s
        return small_u[base : base + 8, rs * 128 : rs * 128 + 128]

    for s in range(2):
        for r in range(4):
            m2_send[s, 8 * r : 8 * r + 8, :] = part(8, r, s)
        m2_send[s, 32:40, :] = jnp.broadcast_to(stf_ref[s : s + 1, :], (8, 128))
    line_start = start_ref[...]
    line_end = line_start + length_ref[...]

    def masked(faces, pos):
        return jnp.where((pos >= line_start) & (pos + 1 < line_end), faces, 0.0)

    face = [masked(stf_ref[s : s + 1, :], 2 * me + s) for s in range(2)]
    lane1 = iota((1, 128), 1)
    normal_face = [jnp.where(lane1 < 127, nof_ref[s : s + 1, :], 0.0) for s in range(2)]
    normal_left = [jnp.where(lane1 > 0, pltpu.roll(normal_face[s], 1, 1), 0.0) for s in range(2)]
    span_face = [spf_send[s : s + 1, :] for s in range(2)]
    local_t = jnp.concatenate([basis, dot3(cn_ref[...], basis, 0, 0)], axis=0)
    outer_t = jnp.concatenate([dot3(cs_ref[...], basis, 0, 0), side_p, jnp.zeros((8, 128), F32)], axis=0)
    pad_rows = jnp.zeros((32, 128), F32)
    turned_t = jnp.transpose(jnp.concatenate([local_t, outer_t], axis=0))[:80]
    local_weights = split(turned_t[:, 0:160])
    outer_weights = split(jnp.transpose(jnp.concatenate([outer_t, pad_rows], axis=0))[:80, 0:96])

    def apply(pair, rows):
        high, low = split(rows)
        both = dot(jnp.concatenate(pair, axis=0), high)
        return both[:80] + (both[80:] + dot(pair[0], low))

    for load in loads_f:
        load.wait()
    for c in range(2):
        columns = []
        for rs in range(4 * c, 4 * c + 4):
            s = rs % 2
            u = u_buf[rs]
            columns.append(
                jnp.concatenate(
                    [
                        f_buf[rs],
                        normal_left[s] * pltpu.roll(u, 1, 1) + normal_face[s] * pltpu.roll(u, 127, 1),
                    ],
                    axis=0,
                )
            )
        modal_buf[c] = apply(local_weights, jnp.concatenate(columns, axis=1))

    pl.semaphore_wait(barrier, count + 1)

    halos = []
    for c in range(2):
        for k, (side, buf) in enumerate(((sp_right, ul_buf), (sp_left, ur_buf))):
            halo = pltpu.make_async_remote_copy(
                u_buf.at[pl.ds(4 * c, 4)],
                buf.at[pl.ds(4 * c, 4)],
                halo_send_sem.at[2 * c + k],
                halo_recv_sem.at[2 * c + k],
                device_id={"span": side},
                device_id_type=MESH,
            )
            if c == 0 and k == 0:
                spf_halo = pltpu.make_async_remote_copy(
                    spf_send, spl_recv, tiny_send_sem.at[0], tiny_recv_sem.at[0],
                    device_id={"span": sp_right}, device_id_type=MESH,
                )
                spf_halo.start()
            halo.start()
            halos.append(halo)

    m2_halos = [
        pltpu.make_async_remote_copy(
            m2_send.at[1 - k], buf, tiny_send_sem.at[1 + k], tiny_recv_sem.at[1 + k],
            device_id={"stream": side}, device_id_type=MESH,
        )
        for k, (side, buf) in enumerate(((st_right, m2l_recv), (st_left, m2r_recv)))
    ]
    for halo in m2_halos:
        halo.start()

    spf_halo.wait_recv()
    span_left = [spl_recv[s : s + 1, :] for s in range(2)]
    diag = [
        pse_ref[s : s + 1, :] + span_left[s] + span_face[s] + normal_left[s] + normal_face[s]
        for s in range(2)
    ]

    lane64 = iota((64, 128), 1)
    first_line = ((lane64 // 32) % 2) == 0
    low_half = lane64 < 64
    perm2 = jnp.concatenate([perm, perm], axis=1)
    perm3 = jnp.concatenate([perm, perm, perm], axis=1)
    h_rows = jnp.concatenate([part(16, r, s) for s in range(2) for l in range(2) for r in range(4)], axis=0)
    c_rows = jnp.concatenate(
        [
            jnp.broadcast_to((diag, face)[q][s], (16, 128))
            for s in range(2)
            for l in range(2)
            for q in range(2)
        ],
        axis=0,
    )
    e_flat = e_send.reshape(64 * 8, 128)
    by_slot = dot(perm2, jnp.concatenate(split(h_rows), axis=1), 1, 1)
    e_flat[pl.ds(0, 64, stride=8), :] = jnp.where(first_line, by_slot[:64], by_slot[64:])
    by_slot = dot(perm3, jnp.concatenate(split3(c_rows), axis=1), 1, 1)
    e_flat[pl.ds(1, 64, stride=8), :] = jnp.where(first_line, by_slot[:64], by_slot[64:])

    def send_all(src, dst, rows, send_sem, recv_sem):
        def one(i, carry):
            peer = peer_of(i)
            pltpu.make_async_remote_copy(
                src.at[peer, pl.ds(0, rows)],
                dst.at[me, pl.ds(0, rows)],
                send_sem,
                recv_sem,
                device_id={"stream": peer},
                device_id_type=MESH,
            ).start()
            return carry

        lax.fori_loop(0, count - 1, one, 0, unroll=9)

    def wait_all(buf, rows, sem):
        blocks = buf.at[pl.ds(0, 63), pl.ds(0, rows)]
        pltpu.make_async_copy(blocks, blocks, sem).wait()

    send_all(e_send, e_recv, 2, e_sems.at[0], e_sems.at[1])
    e_recv[me] = e_send[me]

    for halo in m2_halos:
        halo.wait_recv()
    face_left = [masked(m2l_recv[32:33, :], 2 * me - 1), face[0]]

    for c in range(2):
        halos[2 * c].wait_recv()
        halos[2 * c + 1].wait_recv()
        columns = []
        for r in (2 * c, 2 * c + 1):
            for s in range(2):
                rs = 2 * r + s
                before = m2l_recv[8 * r : 8 * r + 8, :] if s == 0 else part(8, r, 0)
                after = part(8, r, 1) if s == 0 else m2r_recv[8 * r : 8 * r + 8, :]
                columns.append(
                    jnp.concatenate(
                        [
                            span_left[s] * ul_buf[rs] + span_face[s] * ur_buf[rs],
                            (face_left[s] + face[s]) * part(0, r, s) - face_left[s] * before - face[s] * after,
                            jnp.zeros((8, 128), F32),
                        ],
                        axis=0,
                    )
                )
        modal = modal_buf[c] + apply(outer_weights, jnp.concatenate(columns, axis=1))
        modal_high, modal_low = split(modal)
        g_flat = g_send.at[c].reshape(64 * 8, 128)
        for kg in range(5):
            rows = [
                jnp.concatenate(
                    [
                        half[kg * 16 : kg * 16 + 16, (2 * r + s) * 128 : (2 * r + s) * 128 + 128]
                        for s in range(2)
                        for l in range(2)
                        for r in range(2)
                    ],
                    axis=0,
                )
                for half in (modal_high, modal_low)
            ]
            by_slot = dot(perm2, jnp.concatenate(rows, axis=1), 1, 1)
            g_flat[pl.ds(kg, 64, stride=8), :] = jnp.where(first_line, by_slot[:64], by_slot[64:])
        send_all(g_send.at[c], g_recv.at[c], 5, gs_sem.at[c], gr_sem.at[c])
        g_recv[c, me] = g_send[c, me]

    lam_groups = jnp.where((iota((8, 128), 1) // 16) == row8, lam_row, 0.0)
    spread = jnp.where((row % 16) == (lane % 16), 1.0, 0.0).astype(BF16)
    lam_h, lam_m, lam_l = split3(lam_groups)
    rate = dot(lam_h, spread) + dot(lam_m, spread) + dot(lam_l, spread)
    rate_abs = jnp.abs(rate)
    wait_all(e_recv, 2, e_sems.at[1])
    e_got = e_recv.reshape(64 * 8, 128)
    coeffs = e_got[pl.ds(1, 64, stride=8), :]
    even_group = ((lane64 // 16) % 2) == 0
    d_both = jnp.where(even_group, coeffs, pltpu.roll(coeffs, 16, 1))
    f_both = jnp.where(even_group, pltpu.roll(coeffs, 112, 1), coeffs)
    f_swap = pltpu.roll(f_both, 64, 1)
    da_buf[...] = d_both
    db_buf[...] = pltpu.roll(d_both, 64, 1)
    f0_buf[...] = jnp.where(low_half, f_both, f_swap)
    f1_buf[0:8, :] = jnp.zeros((8, 128), F32)
    f1_buf[pl.ds(8, 64), :] = jnp.where(low_half, f_swap, f_both)
    low1 = lane1 < 64
    low8 = iota((8, 128), 1) < 64

    def factor_step(t, d_row, f_now, f_next, inv_before):
        x = rate * f_now
        main = d_row + rate_abs * (f_now + f_next)
        inv = 1.0 / (main - x * x * inv_before)
        inv_buf[t] = inv
        a_buf[t] = x * inv
        b_buf[t] = rate * f_next * inv
        return inv

    def factor(p, inv):
        q = 63 - p
        f_0 = jnp.where(low1, f1_buf[pl.ds(p + 7, 1), :], f1_buf[pl.ds(q + 8, 1), :])
        f_1 = jnp.where(low1, f0_buf[pl.ds(p, 1), :], f0_buf[pl.ds(q, 1), :])
        f_2 = jnp.where(low1, f1_buf[pl.ds(p + 8, 1), :], f1_buf[pl.ds(q + 7, 1), :])
        d_0 = jnp.where(low1, da_buf[pl.ds(p, 1), :], da_buf[pl.ds(q, 1), :])
        d_1 = jnp.where(low1, db_buf[pl.ds(p, 1), :], db_buf[pl.ds(q, 1), :])
        inv = factor_step(2 * p, d_0, f_0, f_1, inv)
        return factor_step(2 * p + 1, d_1, f_1, f_2, inv)

    lax.fori_loop(0, 32, factor, jnp.zeros((8, 128), F32))
    b_last = b_buf[63]
    middle = 1.0 / (1.0 - b_last * pltpu.roll(b_last, 64, 1))

    def turned(rows):
        high = rows.astype(BF16).astype(F32)
        return jnp.transpose(jnp.concatenate([high, rows - high], axis=0)).astype(BF16)

    owner = row - 64 * pair_line
    to_cell = jnp.concatenate(
        [jnp.where(lane == 2 * owner + s, 1.0, 0.0).astype(BF16) for s in range(2)], axis=0
    )
    to_normal = jnp.concatenate([perm[:64], perm[:64], perm[64:], perm[64:]], axis=0)
    h_turned = turned(e_got[pl.ds(0, 64, stride=8), :])
    h_own = dot(jnp.concatenate([h_turned[:64], h_turned[64:]], axis=1), to_cell)
    basis_88 = basis_z[:, 0:88]
    basis_high, basis_low = split(basis_88)
    basis_both = jnp.concatenate([basis_high, basis_low], axis=0)

    def leave_modes(flat, select, lines, side_rows):
        pieces = []
        for kg in range(5):
            t = turned(flat[pl.ds(kg, 64, stride=8), :])
            if lines:
                pair = (jnp.concatenate([t[0:32], t[64:96]], axis=0), jnp.concatenate([t[32:64], t[96:128]], axis=0))
            else:
                pair = (t[:64], t[64:])
            pieces.append(jnp.concatenate(pair, axis=1))
        moved = dot(jnp.concatenate(pieces, axis=0), select)
        columns = [
            jnp.concatenate(
                [moved[kg * 64 + x * 32 + r * 16 : kg * 64 + x * 32 + r * 16 + 16] for kg in range(5)]
                + [side_rows(x, r)],
                axis=0,
            )
            for r in range(2)
            for x in range(2)
        ]
        high, low = split(jnp.concatenate(columns, axis=1))
        both = dot(basis_both, high)
        return both[:80] + (both[80:] + dot(basis_high, low))

    for c in range(2):
        wait_all(g_recv.at[c], 5, gr_sem.at[c])

        d = None
        for p in range(32):
            near = g_recv[c, p]
            far = g_recv[c, 63 - p]
            even = inv_buf[2 * p] * jnp.where(low8, near, far)
            d = even if d is None else even + a_buf[2 * p] * d
            d_buf[2 * p] = d
            odd = pltpu.roll(jnp.where(low8, far, near), 64, 1)
            d = inv_buf[2 * p + 1] * odd + a_buf[2 * p + 1] * d
            d_buf[2 * p + 1] = d
        y = pltpu.roll((d + b_last * pltpu.roll(d, 64, 1)) * middle, 64, 1)
        for p in reversed(range(32)):
            y_odd = d_buf[2 * p + 1] + b_buf[2 * p + 1] * y
            y = d_buf[2 * p] + b_buf[2 * p] * y_odd
            swapped = pltpu.roll(y_odd, 64, 1)
            y_send[c, p] = jnp.where(low8, y, swapped)
            y_send[c, 63 - p] = jnp.where(low8, swapped, y)
        send_all(y_send.at[c], y_recv.at[c], 5, ys_sem.at[c], yr_sem.at[c])
        y_recv[c, me] = y_send[c, me]
    for c in range(2):
        left = leave_modes(
            y_send.at[c].reshape(64 * 8, 128),
            to_cell,
            False,
            lambda x, r, c=c: h_own[x * 32 + (2 * c + r) * 8 : x * 32 + (2 * c + r) * 8 + 8],
        )
        for r in range(2):
            for x in range(2):
                at = (2 * c + r) * 2 + x
                out_ls[at] = left[:, (2 * r + x) * 128 : (2 * r + x) * 128 + 128]
    for c in range(2):
        wait_all(y_recv.at[c], 5, yr_sem.at[c])
        left = leave_modes(
            y_recv.at[c].reshape(64 * 8, 128), to_normal, True, lambda x, r, c=c: part(16, 2 * c + r, x)
        )
        for r in range(2):
            for x in range(2):
                at = (2 * c + r) * 2 + x
                out_rel[at] = left[:, (2 * r + x) * 128 : (2 * r + x) * 128 + 128]

    spf_halo.wait_send()
    for halo in m2_halos:
        halo.wait_send()
    for halo in halos:
        halo.wait_send()
    wait_all(e_send, 2, e_sems.at[0])
    for c in range(2):
        wait_all(g_send.at[c], 5, gs_sem.at[c])
        wait_all(y_send.at[c], 5, ys_sem.at[c])


def store(rel, lines, out_rel, out_ls, sem):
    copies = []
    for at in range(8):
        for k, (src, dst) in enumerate(((rel, out_rel), (lines, out_ls))):
            copies.append(pltpu.make_async_copy(src.at[at], dst.at[:, at // 2, at % 2, 0, :], sem.at[8 * k + at]))
    for copy in copies:
        copy.start()
    for copy in copies:
        copy.wait()


def per_device(
    solution, forcing, pseudo_shift, stream_faces, span_faces, normal_faces, coupling_span, coupling_normal,
    reflectors, eigenvalues, line_start, line_length, line_order,
):
    vmem = pl.BlockSpec(memory_space=pltpu.VMEM)
    hbm = pl.BlockSpec(memory_space=pltpu.HBM)
    block = pltpu.VMEM((8, 80, 128), F32)
    per_peer = pltpu.VMEM((64, 8, 128), F32)
    pair_per_peer = pltpu.VMEM((2, 64, 8, 128), F32)
    two = pltpu.VMEM((2, 128), F32)
    line = pltpu.VMEM((1, 128), jnp.int32)
    dma = pltpu.SemaphoreType.DMA
    out = jax.ShapeDtypeStruct((8, 80, 128), F32)
    relaxed, line_states = pl.pallas_call(
        body,
        out_shape=(out, out),
        in_specs=[hbm] * 13,
        out_specs=(vmem, vmem),
        scratch_shapes=[
            two, two, two, pltpu.VMEM((80, 80), F32), pltpu.VMEM((80, 80), F32),
            pltpu.VMEM((8, 80), F32), pltpu.VMEM((1, 80), F32), line, line, line,
            block, block, block, block,
            two, two,
            pltpu.VMEM((2, 40, 128), F32), pltpu.VMEM((40, 128), F32), pltpu.VMEM((40, 128), F32),
            per_peer, per_peer, pair_per_peer, pair_per_peer, pair_per_peer, pair_per_peer,
            pltpu.VMEM((16, 128), F32),
            pltpu.VMEM((64, 128), F32), pltpu.VMEM((64, 128), F32), pltpu.VMEM((64, 128), F32), pltpu.VMEM((72, 128), F32),
            per_peer, per_peer, per_peer, per_peer, pltpu.VMEM((2, 80, 512), F32),
            dma((27,)), dma((4,)), dma((4,)), dma((3,)), dma((3,)),
            dma((2,)), dma((2,)), dma((2,)), dma((2,)), dma((2,)),
        ],
        compiler_params=pltpu.CompilerParams(
            collective_id=0, has_side_effects=True, vmem_limit_bytes=48 << 20
        ),
        name="relax",
    )(*(pltpu.with_memory_space_constraint(a, pltpu.HBM) for a in (
        solution, forcing, pseudo_shift, stream_faces, span_faces, normal_faces,
        coupling_span, coupling_normal, reflectors, eigenvalues.reshape(1, 80), line_start, line_length, line_order,
    )))
    result = jax.ShapeDtypeStruct((80, 4, 2, 1, 128), F32)
    anywhere = pl.BlockSpec(memory_space=pl.ANY)
    relaxed, line_states = pl.pallas_call(
        store,
        out_shape=(result, result),
        in_specs=[anywhere, anywhere],
        out_specs=(hbm, hbm),
        scratch_shapes=[dma((16,))],
        compiler_params=pltpu.CompilerParams(vmem_limit_bytes=48 << 20),
        name="relaxstore",
    )(relaxed, line_states)
    return relaxed, line_states.reshape(80, 4, 2, 128)


def solution(mesh):
    cells = P(None, None, "stream", "span", None)
    weights = P("stream", "span", None)
    tiles = P("span", None)
    return jax.shard_map(
        per_device,
        mesh=mesh,
        in_specs=(cells, cells, weights, weights, weights, weights, P(), P(), P(), P(), tiles, tiles, tiles),
        out_specs=(cells, P(None, None, ("span", "stream"), None)),
        check_vma=False,
    )
```

```python
import functools

import jax
import jax.numpy as jnp
from jax import lax
from jax.experimental import pallas as pl
from jax.experimental.pallas import tpu as pltpu
from jax.sharding import PartitionSpec as P

F32 = jnp.float32
BF16 = jnp.bfloat16
MESH = pl.DeviceIdType.MESH
EPS = 1e-06


def iota(shape, dim):
    return lax.broadcasted_iota(jnp.int32, shape, dim)


def split(x):
    high = x.astype(BF16)
    return high, (x - high.astype(F32)).astype(BF16)


def split3(x):
    high = x.astype(BF16)
    rest = x - high.astype(F32)
    mid = rest.astype(BF16)
    return high, mid, (rest - mid.astype(F32)).astype(BF16)


def dot(a, b, ca=1, cb=0):
    return lax.dot_general(a, b, (((ca,), (cb,)), ((), ())), preferred_element_type=F32)


def dot3(a, b, ca=1, cb=0):
    ah, al = split(a)
    bh, bl = split(b)
    return dot(ah, bh, ca, cb) + (dot(al, bh, ca, cb) + dot(ah, bl, ca, cb))


def body(
    sol, frc, pse, stf, spf, nof, cs, cn, reflectors, lam, start, length, order,
    out_rel, out_ls,
    pse_ref, stf_ref, nof_ref, cs_ref, cn_ref, refl_ref, lam_ref, start_ref, length_ref, order_ref,
    u_buf, ul_buf, ur_buf, f_buf, spf_send, spl_recv, m2_send, m2l_recv, m2r_recv,
    e_send, e_recv, g_send, g_recv, y_send, y_recv,
    pad_buf, da_buf, db_buf, f0_buf, f1_buf, inv_buf, a_buf, b_buf, d_buf, modal_buf,
    loc_sem, halo_send_sem, halo_recv_sem, tiny_send_sem, tiny_recv_sem,
    e_sems, gs_sem, gr_sem, ys_sem, yr_sem,
):
    me = lax.axis_index("stream")
    count = lax.axis_size("stream")
    sp = lax.axis_index("span")
    sp_count = lax.axis_size("span")
    sp_left = lax.rem(sp + sp_count - 1, sp_count)
    sp_right = lax.rem(sp + 1, sp_count)
    st_left = lax.rem(me + count - 1, count)
    st_right = lax.rem(me + 1, count)


    def peer_of(i):
        jz, jy = i // 8, lax.rem(i, 8)
        dy = 8 + (4 + ((jy + 1) // 2) * (1 - 2 * lax.rem(jy, 2)))
        dz = 8 + (4 + ((jz + 1) // 2) * (1 - 2 * lax.rem(jz, 2)))
        return lax.rem(me // 8 + dy, 8) * 8 + lax.rem(lax.rem(me, 8) + dz, 8)

    g_recv[...] = jnp.zeros_like(g_recv)
    barrier = pltpu.get_barrier_semaphore()
    for side in (sp_left, sp_right):
        pl.semaphore_signal(barrier, inc=1, device_id={"span": side}, device_id_type=MESH)

    def greet(i, carry):
        pl.semaphore_signal(
            barrier, inc=1, device_id={"stream": peer_of(i)}, device_id_type=MESH
        )
        return carry

    lax.fori_loop(0, count - 1, greet, 0, unroll=9)

    loads_u = [
        pltpu.make_async_copy(sol.at[:, rs // 2, rs % 2, 0, :], u_buf.at[rs], loc_sem.at[rs]) for rs in range(8)
    ]
    loads_f = [
        pltpu.make_async_copy(frc.at[:, rs // 2, rs % 2, 0, :], f_buf.at[rs], loc_sem.at[8 + rs]) for rs in range(8)
    ]
    first = ((order, order_ref), (spf.at[:, 0], spf_send), (reflectors, refl_ref), (lam, lam_ref))
    later = (
        (cs, cs_ref), (cn, cn_ref), (pse.at[:, 0], pse_ref), (stf.at[:, 0], stf_ref), (nof.at[:, 0], nof_ref),
        (start, start_ref), (length, length_ref),
    )
    loads_small = [
        pltpu.make_async_copy(src, dst, loc_sem.at[16 + i]) for i, (src, dst) in enumerate(first + later)
    ]
    for load in loads_small[:4]:
        load.start()
    for load in loads_u:
        load.start()
    for load in loads_small[4:]:
        load.start()
    for load in loads_f:
        load.start()


    for load in loads_small[:4]:
        load.wait()

    lane = iota((128, 128), 1)
    row = iota((128, 128), 0)
    perm_t = jnp.where(row == order_ref[...], 1.0, 0.0).astype(BF16)
    pair_line = row // 64
    pick = jnp.where(lane == 2 * (row - 64 * pair_line) + pair_line, 1.0, 0.0).astype(BF16)
    perm = dot(pick, perm_t, 1, 1).astype(BF16)

    for load in loads_small[4:]:
        load.wait()

    pad_buf[...] = jnp.zeros_like(pad_buf)
    pad_buf[0:8, 0:80] = refl_ref[...]
    pad_buf[8:9, 0:80] = lam_ref[...]
    refl = pad_buf[0:8, :]
    lam_row = pad_buf[8:9, :]
    norms = jnp.sum(refl * refl, axis=1, keepdims=True)
    factors = 2.0 / (norms + EPS)
    scales = 2.0 * (EPS**0.5) / (norms + EPS)
    lane80 = iota((80, 128), 1)
    row8 = iota((8, 128), 0)
    basis = jnp.where(iota((80, 128), 0) == lane80, 1.0, 0.0)
    side_z = jnp.zeros((80, 128), F32)
    side_p = jnp.zeros((8, 128), F32)
    for k in range(8):
        w = refl[k : k + 1, :]
        factor = factors[k : k + 1, :]
        z = jnp.sum(basis * w, axis=1, keepdims=True)
        basis = basis - (factor * z) * w
        side_z = jnp.where(lane80 == 80 + k, z * scales[k : k + 1, :], side_z)
        side_p = side_p - (factor * jnp.sum(side_p * w, axis=1, keepdims=True)) * w
        side_p = jnp.where(row8 == k, w, side_p)
    side_p = side_p * scales
    basis_z = basis + side_z
    zt = jnp.transpose(jnp.concatenate([basis_z, jnp.zeros((48, 128), F32)], axis=0))[80:88, 0:80]
    m1 = dot3(side_p * jnp.abs(lam_row), basis, 1, 1)
    m2 = dot3(side_p * lam_row, basis, 1, 1)
    small = jnp.concatenate([m1, m2, zt], axis=0)
    for load in loads_u:
        load.wait()
    state = jnp.concatenate([u_buf[rs] for rs in range(8)], axis=1)
    small_u = dot3(small, state)

    def part(base, r, s):
        rs = 2 * r + s
        return small_u[base : base + 8, rs * 128 : rs * 128 + 128]

    for s in range(2):
        for r in range(4):
            m2_send[s, 8 * r : 8 * r + 8, :] = part(8, r, s)
        m2_send[s, 32:40, :] = jnp.broadcast_to(stf_ref[s : s + 1, :], (8, 128))
    line_start = start_ref[...]
    line_end = line_start + length_ref[...]

    def masked(faces, pos):
        return jnp.where((pos >= line_start) & (pos + 1 < line_end), faces, 0.0)

    face = [masked(stf_ref[s : s + 1, :], 2 * me + s) for s in range(2)]
    lane1 = iota((1, 128), 1)
    normal_face = [jnp.where(lane1 < 127, nof_ref[s : s + 1, :], 0.0) for s in range(2)]
    normal_left = [jnp.where(lane1 > 0, pltpu.roll(normal_face[s], 1, 1), 0.0) for s in range(2)]
    span_face = [spf_send[s : s + 1, :] for s in range(2)]
    local_t = jnp.concatenate([basis, dot3(cn_ref[...], basis, 0, 0)], axis=0)
    outer_t = jnp.concatenate([dot3(cs_ref[...], basis, 0, 0), side_p, jnp.zeros((8, 128), F32)], axis=0)
    pad_rows = jnp.zeros((32, 128), F32)
    turned_t = jnp.transpose(jnp.concatenate([local_t, outer_t], axis=0))[:80]
    local_weights = split(turned_t[:, 0:160])
    outer_weights = split(jnp.transpose(jnp.concatenate([outer_t, pad_rows], axis=0))[:80, 0:96])

    def apply(pair, rows):
        high, low = split(rows)
        both = dot(jnp.concatenate(pair, axis=0), high)
        return both[:80] + (both[80:] + dot(pair[0], low))

    for load in loads_f:
        load.wait()
    for c in range(2):
        columns = []
        for rs in range(4 * c, 4 * c + 4):
            s = rs % 2
            u = u_buf[rs]
            columns.append(
                jnp.concatenate(
                    [
                        f_buf[rs],
                        normal_left[s] * pltpu.roll(u, 1, 1) + normal_face[s] * pltpu.roll(u, 127, 1),
                    ],
                    axis=0,
                )
            )
        modal_buf[c] = apply(local_weights, jnp.concatenate(columns, axis=1))

    lane64 = iota((64, 128), 1)
    first_line = ((lane64 // 32) % 2) == 0
    low_half = lane64 < 64
    perm2 = jnp.concatenate([perm, perm], axis=1)
    perm3 = jnp.concatenate([perm, perm, perm], axis=1)
    h_rows = jnp.concatenate([part(16, r, s) for s in range(2) for l in range(2) for r in range(4)], axis=0)
    e_flat = e_send.reshape(64 * 8, 128)
    by_slot = dot(perm2, jnp.concatenate(split(h_rows), axis=1), 1, 1)
    e_flat[pl.ds(0, 64, stride=8), :] = jnp.where(first_line, by_slot[:64], by_slot[64:])
    pl.semaphore_wait(barrier, count + 1)

    halos = []
    for c in range(2):
        for k, (side, buf) in enumerate(((sp_right, ul_buf), (sp_left, ur_buf))):
            halo = pltpu.make_async_remote_copy(
                u_buf.at[pl.ds(4 * c, 4)],
                buf.at[pl.ds(4 * c, 4)],
                halo_send_sem.at[2 * c + k],
                halo_recv_sem.at[2 * c + k],
                device_id={"span": side},
                device_id_type=MESH,
            )
            if c == 0 and k == 0:
                spf_halo = pltpu.make_async_remote_copy(
                    spf_send, spl_recv, tiny_send_sem.at[0], tiny_recv_sem.at[0],
                    device_id={"span": sp_right}, device_id_type=MESH,
                )
                spf_halo.start()
            halo.start()
            halos.append(halo)

    m2_halos = [
        pltpu.make_async_remote_copy(
            m2_send.at[1 - k], buf, tiny_send_sem.at[1 + k], tiny_recv_sem.at[1 + k],
            device_id={"stream": side}, device_id_type=MESH,
        )
        for k, (side, buf) in enumerate(((st_right, m2l_recv), (st_left, m2r_recv)))
    ]
    for halo in m2_halos:
        halo.start()

    spf_halo.wait_recv()
    span_left = [spl_recv[s : s + 1, :] for s in range(2)]
    diag = [
        pse_ref[s : s + 1, :] + span_left[s] + span_face[s] + normal_left[s] + normal_face[s]
        for s in range(2)
    ]

    c_rows = jnp.concatenate(
        [
            jnp.broadcast_to((diag, face)[q][s], (16, 128))
            for s in range(2)
            for l in range(2)
            for q in range(2)
        ],
        axis=0,
    )
    by_slot = dot(perm3, jnp.concatenate(split3(c_rows), axis=1), 1, 1)
    e_flat[pl.ds(1, 64, stride=8), :] = jnp.where(first_line, by_slot[:64], by_slot[64:])

    def send_all(src, dst, rows, send_sem, recv_sem):
        def one(i, carry):
            peer = peer_of(i)
            pltpu.make_async_remote_copy(
                src.at[peer, pl.ds(0, rows)],
                dst.at[me, pl.ds(0, rows)],
                send_sem,
                recv_sem,
                device_id={"stream": peer},
                device_id_type=MESH,
            ).start()
            return carry

        lax.fori_loop(0, count - 1, one, 0, unroll=9)

    def wait_all(buf, rows, sem):
        blocks = buf.at[pl.ds(0, 63), pl.ds(0, rows)]
        pltpu.make_async_copy(blocks, blocks, sem).wait()

    send_all(e_send, e_recv, 2, e_sems.at[0], e_sems.at[1])
    e_recv[me] = e_send[me]

    for halo in m2_halos:
        halo.wait_recv()
    face_left = [masked(m2l_recv[32:33, :], 2 * me - 1), face[0]]

    for c in range(2):
        halos[2 * c].wait_recv()
        halos[2 * c + 1].wait_recv()
        columns = []
        for r in (2 * c, 2 * c + 1):
            for s in range(2):
                rs = 2 * r + s
                before = m2l_recv[8 * r : 8 * r + 8, :] if s == 0 else part(8, r, 0)
                after = part(8, r, 1) if s == 0 else m2r_recv[8 * r : 8 * r + 8, :]
                columns.append(
                    jnp.concatenate(
                        [
                            span_left[s] * ul_buf[rs] + span_face[s] * ur_buf[rs],
                            (face_left[s] + face[s]) * part(0, r, s) - face_left[s] * before - face[s] * after,
                            jnp.zeros((8, 128), F32),
                        ],
                        axis=0,
                    )
                )
        modal = modal_buf[c] + apply(outer_weights, jnp.concatenate(columns, axis=1))
        modal_high, modal_low = split(modal)
        g_flat = g_send.at[c].reshape(64 * 8, 128)
        for kg in range(5):
            rows = [
                jnp.concatenate(
                    [
                        half[kg * 16 : kg * 16 + 16, (2 * r + s) * 128 : (2 * r + s) * 128 + 128]
                        for s in range(2)
                        for l in range(2)
                        for r in range(2)
                    ],
                    axis=0,
                )
                for half in (modal_high, modal_low)
            ]
            by_slot = dot(perm2, jnp.concatenate(rows, axis=1), 1, 1)
            g_flat[pl.ds(kg, 64, stride=8), :] = jnp.where(first_line, by_slot[:64], by_slot[64:])
        send_all(g_send.at[c], g_recv.at[c], 5, gs_sem.at[c], gr_sem.at[c])
        g_recv[c, me] = g_send[c, me]

    lam_groups = jnp.where((iota((8, 128), 1) // 16) == row8, lam_row, 0.0)
    spread = jnp.where((row % 16) == (lane % 16), 1.0, 0.0).astype(BF16)
    lam_h, lam_m, lam_l = split3(lam_groups)
    rate = dot(lam_h, spread) + dot(lam_m, spread) + dot(lam_l, spread)
    rate_abs = jnp.abs(rate)
    wait_all(e_recv, 2, e_sems.at[1])
    e_got = e_recv.reshape(64 * 8, 128)
    coeffs = e_got[pl.ds(1, 64, stride=8), :]
    even_group = ((lane64 // 16) % 2) == 0
    d_both = jnp.where(even_group, coeffs, pltpu.roll(coeffs, 16, 1))
    f_both = jnp.where(even_group, pltpu.roll(coeffs, 112, 1), coeffs)
    f_swap = pltpu.roll(f_both, 64, 1)
    da_buf[...] = d_both
    db_buf[...] = pltpu.roll(d_both, 64, 1)
    f0_buf[...] = jnp.where(low_half, f_both, f_swap)
    f1_buf[0:8, :] = jnp.zeros((8, 128), F32)
    f1_buf[pl.ds(8, 64), :] = jnp.where(low_half, f_swap, f_both)
    low1 = lane1 < 64
    low8 = iota((8, 128), 1) < 64

    def factor_step(t, d_row, f_now, f_next, inv_before):
        x = rate * f_now
        main = d_row + rate_abs * (f_now + f_next)
        inv = 1.0 / (main - x * x * inv_before)
        inv_buf[t] = inv
        a_buf[t] = x * inv
        b_buf[t] = rate * f_next * inv
        return inv

    def factor(p, inv):
        q = 63 - p
        f_0 = jnp.where(low1, f1_buf[pl.ds(p + 7, 1), :], f1_buf[pl.ds(q + 8, 1), :])
        f_1 = jnp.where(low1, f0_buf[pl.ds(p, 1), :], f0_buf[pl.ds(q, 1), :])
        f_2 = jnp.where(low1, f1_buf[pl.ds(p + 8, 1), :], f1_buf[pl.ds(q + 7, 1), :])
        d_0 = jnp.where(low1, da_buf[pl.ds(p, 1), :], da_buf[pl.ds(q, 1), :])
        d_1 = jnp.where(low1, db_buf[pl.ds(p, 1), :], db_buf[pl.ds(q, 1), :])
        inv = factor_step(2 * p, d_0, f_0, f_1, inv)
        return factor_step(2 * p + 1, d_1, f_1, f_2, inv)

    lax.fori_loop(0, 32, factor, jnp.zeros((8, 128), F32), unroll=8)
    b_last = b_buf[63]
    middle = 1.0 / (1.0 - b_last * pltpu.roll(b_last, 64, 1))

    def turned(rows):
        high = rows.astype(BF16).astype(F32)
        return jnp.transpose(jnp.concatenate([high, rows - high], axis=0)).astype(BF16)

    owner = row - 64 * pair_line
    to_cell = jnp.concatenate(
        [jnp.where(lane == 2 * owner + s, 1.0, 0.0).astype(BF16) for s in range(2)], axis=0
    )
    to_normal = jnp.concatenate([perm[:64], perm[:64], perm[64:], perm[64:]], axis=0)
    h_turned = turned(e_got[pl.ds(0, 64, stride=8), :])
    h_own = dot(jnp.concatenate([h_turned[:64], h_turned[64:]], axis=1), to_cell)
    basis_88 = basis_z[:, 0:88]
    basis_high, basis_low = split(basis_88)
    basis_both = jnp.concatenate([basis_high, basis_low], axis=0)

    def leave_modes(flat, select, lines, side_rows):
        pieces = []
        for kg in range(5):
            t = turned(flat[pl.ds(kg, 64, stride=8), :])
            if lines:
                pair = (jnp.concatenate([t[0:32], t[64:96]], axis=0), jnp.concatenate([t[32:64], t[96:128]], axis=0))
            else:
                pair = (t[:64], t[64:])
            pieces.append(jnp.concatenate(pair, axis=1))
        moved = dot(jnp.concatenate(pieces, axis=0), select)
        columns = [
            jnp.concatenate(
                [moved[kg * 64 + x * 32 + r * 16 : kg * 64 + x * 32 + r * 16 + 16] for kg in range(5)]
                + [side_rows(x, r)],
                axis=0,
            )
            for r in range(2)
            for x in range(2)
        ]
        high, low = split(jnp.concatenate(columns, axis=1))
        both = dot(basis_both, high)
        return both[:80] + (both[80:] + dot(basis_high, low))

    for c in range(2):
        wait_all(g_recv.at[c], 5, gr_sem.at[c])

        d = None
        for p in range(32):
            near = g_recv[c, p]
            far = g_recv[c, 63 - p]
            even = inv_buf[2 * p] * jnp.where(low8, near, far)
            d = even if d is None else even + a_buf[2 * p] * d
            d_buf[2 * p] = d
            odd = pltpu.roll(jnp.where(low8, far, near), 64, 1)
            d = inv_buf[2 * p + 1] * odd + a_buf[2 * p + 1] * d
            d_buf[2 * p + 1] = d
        y = pltpu.roll((d + b_last * pltpu.roll(d, 64, 1)) * middle, 64, 1)
        for p in reversed(range(32)):
            y_odd = d_buf[2 * p + 1] + b_buf[2 * p + 1] * y
            y = d_buf[2 * p] + b_buf[2 * p] * y_odd
            swapped = pltpu.roll(y_odd, 64, 1)
            y_send[c, p] = jnp.where(low8, y, swapped)
            y_send[c, 63 - p] = jnp.where(low8, swapped, y)
        send_all(y_send.at[c], y_recv.at[c], 5, ys_sem.at[c], yr_sem.at[c])
        y_recv[c, me] = y_send[c, me]
    for c in range(2):
        left = leave_modes(
            y_send.at[c].reshape(64 * 8, 128),
            to_cell,
            False,
            lambda x, r, c=c: h_own[x * 32 + (2 * c + r) * 8 : x * 32 + (2 * c + r) * 8 + 8],
        )
        for r in range(2):
            for x in range(2):
                at = (2 * c + r) * 2 + x
                out_ls[at] = left[:, (2 * r + x) * 128 : (2 * r + x) * 128 + 128]
    for c in range(2):
        wait_all(y_recv.at[c], 5, yr_sem.at[c])
        left = leave_modes(
            y_recv.at[c].reshape(64 * 8, 128), to_normal, True, lambda x, r, c=c: part(16, 2 * c + r, x)
        )
        for r in range(2):
            for x in range(2):
                at = (2 * c + r) * 2 + x
                out_rel[at] = left[:, (2 * r + x) * 128 : (2 * r + x) * 128 + 128]

    spf_halo.wait_send()
    for halo in m2_halos:
        halo.wait_send()
    for halo in halos:
        halo.wait_send()
    wait_all(e_send, 2, e_sems.at[0])
    for c in range(2):
        wait_all(g_send.at[c], 5, gs_sem.at[c])
        wait_all(y_send.at[c], 5, ys_sem.at[c])


def store(rel, lines, out_rel, out_ls, sem):
    copies = []
    for at in range(8):
        for k, (src, dst) in enumerate(((rel, out_rel), (lines, out_ls))):
            copies.append(pltpu.make_async_copy(src.at[at], dst.at[:, at // 2, at % 2, 0, :], sem.at[8 * k + at]))
    for copy in copies:
        copy.start()
    for copy in copies:
        copy.wait()


def per_device(
    solution, forcing, pseudo_shift, stream_faces, span_faces, normal_faces, coupling_span, coupling_normal,
    reflectors, eigenvalues, line_start, line_length, line_order,
):
    vmem = pl.BlockSpec(memory_space=pltpu.VMEM)
    hbm = pl.BlockSpec(memory_space=pltpu.HBM)
    block = pltpu.VMEM((8, 80, 128), F32)
    per_peer = pltpu.VMEM((64, 8, 128), F32)
    pair_per_peer = pltpu.VMEM((2, 64, 8, 128), F32)
    two = pltpu.VMEM((2, 128), F32)
    line = pltpu.VMEM((1, 128), jnp.int32)
    dma = pltpu.SemaphoreType.DMA
    out = jax.ShapeDtypeStruct((8, 80, 128), F32)
    relaxed, line_states = pl.pallas_call(
        body,
        out_shape=(out, out),
        in_specs=[hbm] * 13,
        out_specs=(vmem, vmem),
        scratch_shapes=[
            two, two, two, pltpu.VMEM((80, 80), F32), pltpu.VMEM((80, 80), F32),
            pltpu.VMEM((8, 80), F32), pltpu.VMEM((1, 80), F32), line, line, line,
            block, block, block, block,
            two, two,
            pltpu.VMEM((2, 40, 128), F32), pltpu.VMEM((40, 128), F32), pltpu.VMEM((40, 128), F32),
            per_peer, per_peer, pair_per_peer, pair_per_peer, pair_per_peer, pair_per_peer,
            pltpu.VMEM((16, 128), F32),
            pltpu.VMEM((64, 128), F32), pltpu.VMEM((64, 128), F32), pltpu.VMEM((64, 128), F32), pltpu.VMEM((72, 128), F32),
            per_peer, per_peer, per_peer, per_peer, pltpu.VMEM((2, 80, 512), F32),
            dma((27,)), dma((4,)), dma((4,)), dma((3,)), dma((3,)),
            dma((2,)), dma((2,)), dma((2,)), dma((2,)), dma((2,)),
        ],
        compiler_params=pltpu.CompilerParams(
            collective_id=0, has_side_effects=True, vmem_limit_bytes=48 << 20
        ),
        name="relax",
    )(*(pltpu.with_memory_space_constraint(a, pltpu.HBM) for a in (
        solution, forcing, pseudo_shift, stream_faces, span_faces, normal_faces,
        coupling_span, coupling_normal, reflectors, eigenvalues.reshape(1, 80), line_start, line_length, line_order,
    )))
    result = jax.ShapeDtypeStruct((80, 4, 2, 1, 128), F32)
    anywhere = pl.BlockSpec(memory_space=pl.ANY)
    relaxed, line_states = pl.pallas_call(
        store,
        out_shape=(result, result),
        in_specs=[anywhere, anywhere],
        out_specs=(hbm, hbm),
        scratch_shapes=[dma((16,))],
        compiler_params=pltpu.CompilerParams(vmem_limit_bytes=48 << 20),
        name="relaxstore",
    )(relaxed, line_states)
    return relaxed, line_states.reshape(80, 4, 2, 128)


def solution(mesh):
    cells = P(None, None, "stream", "span", None)
    weights = P("stream", "span", None)
    tiles = P("span", None)
    return jax.shard_map(
        per_device,
        mesh=mesh,
        in_specs=(cells, cells, weights, weights, weights, weights, P(), P(), P(), P(), tiles, tiles, tiles),
        out_specs=(cells, P(None, None, ("span", "stream"), None)),
        check_vma=False,
    )
```
